128 devices in a mesh: dp: 8 (over z, core), mp: 16 (over y, x).
Axes of the slice: x: 4, y: 4, z: 4, core: 2. Of those that a mesh axis runs over, the one named last changes fastest.
Arguments:
- gradient: bfloat16 [80, 262144], P(None, ('dp', 'mp')), may hold values from -1500 to 1500
- owner_device: int32 [80], replicated, may hold values from 0 to 127, as said below
- state_slot: int32 [80], replicated, may hold values from 0 to 1
- left_stat: float32 [256, 512, 512], P(('dp', 'mp')), may hold values from -8 to 10, as said below
- right_stat: float32 [256, 512, 512], P(('dp', 'mp')), may hold values from -8 to 10, as said below
- left_basis: float32 [256, 512, 512], P(('dp', 'mp')), may hold values from -1 to 1, as said below
- right_basis: float32 [256, 512, 512], P(('dp', 'mp')), may hold values from -1 to 1, as said below
- moment: float32 [256, 512, 512], P(('dp', 'mp')), may hold values from -4 to 4
- second_moment: float32 [256, 512, 512], P(('dp', 'mp')), may hold values from 0.2 to 5
Outputs:
- new_left_stat: float32 [256, 512, 512], P(('dp', 'mp'))
- new_right_stat: float32 [256, 512, 512], P(('dp', 'mp'))
- new_left_basis: float32 [256, 512, 512], P(('dp', 'mp'))
- new_right_basis: float32 [256, 512, 512], P(('dp', 'mp'))
- new_moment: float32 [256, 512, 512], P(('dp', 'mp'))
- new_second_moment: float32 [256, 512, 512], P(('dp', 'mp'))
- direction: float32 [80, 262144], P(None, ('dp', 'mp'))
The draws below stay inside these ranges and needn't reach their ends.
Inputs may be any that keep to these rules, and one draw needn't show every extreme that they name: Block b's state is slot state_slot[b] of device owner_device[b], devices counted in dp+mp order; no two blocks share a slot. Devices 2k and 2k + 1 hold at most 2 blocks together, the first two and the last two devices hold one block each, and some devices hold 2. `left_stat`: symmetric positive definite. `right_stat`: symmetric positive definite. `left_basis`: orthogonal matrices. `right_basis`: orthogonal matrices.
All inputs are finite; a program needn't handle non-finite values.
Results may differ from the reference program's by a relative error of at most 0.0003.
Values may be sent and summed in bfloat16 or wider, within the bound.
A program may use at most 128 MiB of HBM per device.

```python
import math
import jax
import jax.numpy as jnp
from jax import lax

B = 512
CAP = 2
OWNERS = 128
BLOCKS = 80
ALL_SLOTS = 256


def slot_table(key):
    pair_count = OWNERS // 2
    quarter = pair_count // 4
    pair_kinds = jnp.concatenate([jnp.zeros((quarter,), jnp.int32), jnp.ones((quarter - 2,), jnp.int32), jnp.full((quarter,), 2, jnp.int32), jnp.full((quarter,), 3, jnp.int32)])
    pair_kinds = jax.random.permutation(jax.random.fold_in(key, 101), pair_kinds)
    pair_kinds = jnp.concatenate([jnp.ones((1,), jnp.int32), pair_kinds, jnp.ones((1,), jnp.int32)])
    heavy_side = jax.random.randint(jax.random.fold_in(key, 102), (pair_count, 1, 1), 0, 2)
    first_slot = jax.random.randint(jax.random.fold_in(key, 103), (pair_count, 1, 1), 0, CAP)
    second_slot = jax.random.randint(jax.random.fold_in(key, 104), (pair_count, 1, 1), 0, CAP)
    member = jnp.arange(2, dtype=jnp.int32)[None, :, None]
    slot_place = jnp.arange(CAP, dtype=jnp.int32)[None, None, :]
    kind_grid = pair_kinds[:, None, None]
    heavy_live = (kind_grid == 0) & (member == heavy_side)
    double_live = (kind_grid == 1) & jnp.where(member == 0, slot_place == first_slot, slot_place == second_slot)
    single_live = (kind_grid == 2) & (member == heavy_side) & (slot_place == first_slot)
    occupied = (heavy_live | double_live | single_live).reshape(-1)
    taken_slots = jnp.nonzero(occupied, size=BLOCKS)[0].astype(jnp.int32)
    shuffle = jax.random.permutation(jax.random.fold_in(key, 105), BLOCKS)
    return taken_slots[shuffle]


def draw_owner_device(key, part):
    shared = slot_table(key)
    return (shared // CAP).astype(jnp.int32)


def draw_state_slot(key, part):
    shared = slot_table(key)
    return (shared % CAP).astype(jnp.int32)


def draw_gradient(key, part):
    key = jax.random.fold_in(key, 3)
    row_scale = 10.0 ** (jnp.arange(B, dtype=jnp.float32) / B)
    column_scale = 10.0 ** jax.random.uniform(jax.random.fold_in(key, 1), (BLOCKS, 1, B), dtype=jnp.float32)
    noise = jnp.clip(jax.random.normal(jax.random.fold_in(key, 3), (BLOCKS, B, B), dtype=jnp.float32), -4.0, 4.0)
    values = noise * row_scale[None, :, None] * column_scale
    return values.reshape(BLOCKS, B * B).astype(jnp.bfloat16)


def spd_stack(key):
    count = OWNERS * CAP
    diagonal = 0.5 * 4.0 ** jax.random.uniform(jax.random.fold_in(key, 1), (count, B, 1), dtype=jnp.float32)
    factor = jnp.clip(jax.random.normal(jax.random.fold_in(key, 2), (count, B, B), dtype=jnp.float32), -4.0, 4.0) / math.sqrt(B)
    product = jnp.matmul(factor, jnp.swapaxes(factor, -1, -2), precision=lax.Precision.HIGHEST)
    return 0.5 * product + diagonal * jnp.eye(B, dtype=jnp.float32)


def orthogonal_stack(key):
    count = OWNERS * CAP
    columns = jnp.broadcast_to(jnp.eye(B, dtype=jnp.float32), (count, B, B))
    for layer in range(8):
        order = jax.random.permutation(jax.random.fold_in(key, 10 + layer), B)
        columns = columns[:, :, order]
        paired = columns.reshape(count, B, B // 2, 2)
        first_col = paired[..., 0]
        second_col = paired[..., 1]
        angles = jax.random.uniform(jax.random.fold_in(key, 30 + layer), (count, 1, B // 2), dtype=jnp.float32, minval=-0.8, maxval=0.8)
        cosine = jnp.cos(angles)
        sine = jnp.sin(angles)
        turned_first = cosine * first_col - sine * second_col
        turned_second = sine * first_col + cosine * second_col
        columns = jnp.stack([turned_first, turned_second], axis=-1).reshape(count, B, B)
    return columns


def draw_left_stat(key, part):
    key = jax.random.fold_in(key, 4)
    return spd_stack(key)


def draw_right_stat(key, part):
    key = jax.random.fold_in(key, 5)
    return spd_stack(key)


def draw_left_basis(key, part):
    key = jax.random.fold_in(key, 6)
    return orthogonal_stack(key)


def draw_right_basis(key, part):
    key = jax.random.fold_in(key, 7)
    return orthogonal_stack(key)


def block_scale(stream_key, shape, split, smallest, largest):
    def one(dim, blocks):
        heights = jax.random.uniform(jax.random.fold_in(jax.random.fold_in(stream_key, 6), dim), (blocks,), jnp.float32, smallest / len(split), largest / len(split))
        return jnp.repeat(jnp.exp(heights), shape[dim] // blocks).reshape((-1,) + (1,) * (len(shape) - dim - 1))

    level = one(*split[0])
    for cut in split[1:]:
        level = level * one(*cut)
    return level


def gaussian(own_key, shape, deviation, reach, pieces=(), held_as=jnp.bfloat16):
    gain = block_scale(own_key, shape, pieces, -0.22, 0.18) if pieces else 1.0
    entries = jax.random.normal(own_key, shape, jnp.float32) * deviation * gain
    return jnp.minimum(jnp.maximum(entries, -reach), reach).astype(held_as)


def setup_inputs(seed: int = 0) -> dict:
    keys = jax.random.split(jax.random.key(seed), 10)
    return {
        "gradient": draw_gradient(jax.random.fold_in(keys[9], 71), 0),
        "owner_device": draw_owner_device(jax.random.fold_in(keys[9], 71), 0),
        "state_slot": draw_state_slot(jax.random.fold_in(keys[9], 71), 0),
        "left_stat": draw_left_stat(jax.random.fold_in(keys[9], 71), 0),
        "right_stat": draw_right_stat(jax.random.fold_in(keys[9], 71), 0),
        "left_basis": draw_left_basis(jax.random.fold_in(keys[9], 71), 0),
        "right_basis": draw_right_basis(jax.random.fold_in(keys[9], 71), 0),
        "moment": gaussian(keys[7], (ALL_SLOTS, B, B), 1.0, 4.0, ((0, 128),), jnp.float32),
        "second_moment": jnp.clip(jnp.exp(math.log(5.0) - 3.218876 * jax.random.uniform(keys[8], (ALL_SLOTS, B, B), jnp.float32) ** block_scale(keys[8], (ALL_SLOTS, B, B), ((0, 128),), -0.2, 0.2)), 0.2, 5.0),
    }


average_decay = 0.9
stability = 1e-08

def exact_dot(left_side, right_side):
    return jnp.matmul(left_side, right_side, precision=lax.Precision.HIGHEST)

def flipped(matrix):
    return jnp.swapaxes(matrix, -1, -2)

def refresh_basis(statistic, old_basis):
    powered = exact_dot(statistic, old_basis)
    gram_matrix = exact_dot(flipped(powered), powered)
    triangle = jnp.linalg.cholesky(gram_matrix)
    return flipped(jax.scipy.linalg.solve_triangular(triangle, flipped(powered), lower=True))

def soap_block(gradient, left_stat, right_stat, left_basis, right_basis, moment, second_moment):
    new_left = average_decay * left_stat + (1.0 - average_decay) / B * exact_dot(gradient, flipped(gradient))
    new_right = average_decay * right_stat + (1.0 - average_decay) / B * exact_dot(flipped(gradient), gradient)
    new_moment = average_decay * moment + (1.0 - average_decay) * gradient
    rotated = exact_dot(exact_dot(flipped(left_basis), gradient), right_basis)
    rotated_moment = exact_dot(exact_dot(flipped(left_basis), new_moment), right_basis)
    new_second = average_decay * second_moment + (1.0 - average_decay) * rotated * rotated
    ratio = rotated_moment / (jnp.sqrt(new_second) + stability)
    step_out = exact_dot(exact_dot(left_basis, ratio), flipped(right_basis))
    return (new_left, new_right, refresh_basis(new_left, left_basis), refresh_basis(new_right, right_basis), new_moment, new_second, step_out)

def reference(gradient, owner_device, state_slot, left_stat, right_stat, left_basis, right_basis, moment, second_moment):
    square_mean = jnp.mean(jnp.square(gradient.astype(jnp.float32)))
    clip_scale = 1.0 / jnp.maximum(1.0, jnp.sqrt(square_mean))
    placed = (owner_device * CAP + state_slot).astype(jnp.int32)

    def one_block(index):
        where_slot = placed[index]
        block_grad = gradient[index].astype(jnp.float32).reshape(B, B) * clip_scale
        return soap_block(block_grad, left_stat[where_slot], right_stat[where_slot], left_basis[where_slot], right_basis[where_slot], moment[where_slot], second_moment[where_slot])
    outcome = lax.map(one_block, jnp.arange(BLOCKS, dtype=jnp.int32))
    previous = (left_stat, right_stat, left_basis, right_basis, moment, second_moment)
    renewed = [previous[number].at[placed].set(outcome[number]) for number in range(6)]
    direction = outcome[6].reshape(BLOCKS, B * B)
    return (renewed[0], renewed[1], renewed[2], renewed[3], renewed[4], renewed[5], direction)
```

```python
import functools

import jax
import jax.numpy as jnp
from jax import lax
from jax.experimental import pallas as pl
from jax.experimental.pallas import tpu as pltpu
from jax.sharding import PartitionSpec as P

average_decay = 0.9
stability = 1e-08

N = 512
D = 128
LB = 32
F32 = jnp.float32
BF16 = jnp.bfloat16


def split(x):
    hi = x.astype(BF16)
    lo = (x - hi.astype(F32)).astype(BF16)
    return hi, lo


def dot3(a, b, ca, cb):
    dims = (((ca,), (cb,)), ((), ()))
    d = lambda x, y: lax.dot_general(x, y, dims, preferred_element_type=F32)
    return d(a[0], b[0]) + (d(a[0], b[1]) + d(a[1], b[0]))


def leaf(ws, s, lb):
    n = len(ws)
    rows = lax.broadcasted_iota(jnp.int32, (lb, 1), 0)
    lanes = lax.broadcasted_iota(jnp.int32, (lb, D), 1)
    for k in range(lb - 1):
        for b in range(n):
            d, e = ws[b]
            c = s * lb + k
            col = d[:, c:c + 1]
            rp = 1.0 / d[k:k + 1, c:c + 1]
            m = jnp.where(rows > k, col, 0.0) * rp
            d = d - m * d[k:k + 1, :]
            e = e - m * e[k:k + 1, :]
            ws[b] = (d, e)
    out = []
    on = lanes == lax.broadcasted_iota(jnp.int32, (lb, D), 0) + s * lb
    for b in range(n):
        d, e = ws[b]
        piv = jnp.sum(jnp.where(on, d, 0.0), axis=1, keepdims=True)
        r = lax.rsqrt(piv)
        out.append((d * r, e * r))
    return out


def factor_body(nm, lb, a_ref, p_ref, q_ref, w_d, w_e):
    eye = (lax.broadcasted_iota(jnp.int32, (D, D), 0) == lax.broadcasted_iota(jnp.int32, (D, D), 1)).astype(F32)

    def step(k, carry):
        at = pl.ds(pl.multiple_of(k * D, D), D)
        for b in range(nm):
            w_d[b] = a_ref[b, at, at]
            w_e[b] = eye
        for s in range(D // lb):
            here = slice(s * lb, (s + 1) * lb)
            ws = [(w_d[b, here, :], w_e[b, here, :]) for b in range(nm)]
            ws = leaf(ws, s, lb)
            for b in range(nm):
                rd, re = ws[b]
                w_e[b, here, :] = re
                if s < D // lb - 1:
                    low = slice((s + 1) * lb, D)
                    dh, dl = split(rd)
                    eh, el = split(re)
                    lhs = jnp.concatenate([dh, dh, dl], axis=0)
                    rhs_d = jnp.concatenate([dh, dl, dh], axis=0)
                    rhs_e = jnp.concatenate([eh, el, eh], axis=0)
                    dims = (((0,), (0,)), ((), ()))
                    ud = lax.dot_general(lhs, rhs_d, dims, preferred_element_type=F32)
                    ue = lax.dot_general(lhs, rhs_e, dims, preferred_element_type=F32)
                    w_d[b, low, :] = w_d[b, low, :] - ud[(s + 1) * lb:, :]
                    w_e[b, low, :] = w_e[b, low, :] - ue[(s + 1) * lb:, :]
        for kk in range(N // D):
            @pl.when(k == kk)
            def _():
                o = kk * D
                for b in range(nm):
                    x = split(w_e[b])
                    q = dot3(split(p_ref[b, :, o:o + D]), x, 1, 1)
                    q_ref[b, :, o:o + D] = q
                    if kk < N // D - 1:
                        r = split(dot3(x, split(a_ref[b, o:o + D, o + D:]), 1, 0))
                        a_ref[b, o + D:, o + D:] = a_ref[b, o + D:, o + D:] - dot3(r, r, 0, 0)
                        p_ref[b, :, o + D:] = p_ref[b, :, o + D:] - dot3(split(q), r, 1, 0)
        return carry

    lax.fori_loop(0, N // D, step, 0)


def refresh_kernel(nm, lb, s_ref, l_ref, q_ref, a_ref, p_ref, w_d, w_e):
    for b in range(nm):
        p = dot3(split(s_ref[b]), split(l_ref[b]), 1, 0)
        p_ref[b] = p
        ps = split(p)
        a_ref[b] = dot3(ps, ps, 0, 0)
    factor_body(nm, lb, a_ref, p_ref, q_ref, w_d, w_e)


def refresh(stat, basis, lb=LB):
    nm = stat.shape[0]
    return pl.pallas_call(
        functools.partial(refresh_kernel, nm, lb),
        out_shape=jax.ShapeDtypeStruct((nm, N, N), F32),
        in_specs=[pl.BlockSpec(memory_space=pltpu.VMEM)] * 2,
        out_specs=pl.BlockSpec(memory_space=pltpu.VMEM),
        scratch_shapes=[
            pltpu.VMEM((nm, N, N), F32),
            pltpu.VMEM((nm, N, N), F32),
            pltpu.VMEM((nm, D, D), F32),
            pltpu.VMEM((nm, D, D), F32),
        ],
        compiler_params=pltpu.CompilerParams(vmem_limit_bytes=56 << 20),
        name="refresh",
    )(stat, basis)


def dot(a, b):
    return jnp.matmul(a, b, precision=lax.Precision.HIGH)


def flipped(matrix):
    return jnp.swapaxes(matrix, -1, -2)


def shards(
    gradient,
    owner_device,
    state_slot,
    left_stat,
    right_stat,
    left_basis,
    right_basis,
    moment,
    second_moment,
):
    devices = lax.axis_size(("dp", "mp"))
    slot_count = left_stat.shape[0]
    block_width = left_stat.shape[-1]
    flat_piece = gradient.shape[1]
    block_count = gradient.shape[0]
    my_index = lax.axis_index(("dp", "mp"))
    own_square = jnp.sum(jnp.square(gradient.astype(F32)))
    first = own_square.astype(BF16)
    second = (own_square - first.astype(F32)).astype(BF16)
    third = (own_square - first.astype(F32) - second.astype(F32)).astype(BF16)
    terms = jnp.stack([first, second, third])
    slot_code = state_slot * devices + owner_device
    picker = (
        slot_code[None, :] == jnp.arange(slot_count * devices, dtype=jnp.int32)[:, None]
    ).astype(BF16)
    outgoing = jnp.dot(picker, gradient, preferred_element_type=F32).astype(BF16)
    outgoing = outgoing.reshape(slot_count, devices, flat_piece)
    tail = jnp.broadcast_to(jnp.pad(terms, (0, 125)), (slot_count, devices, 128))
    outgoing = jnp.concatenate([outgoing, tail], axis=2)
    arrived = lax.all_to_all(outgoing, ("dp", "mp"), split_axis=1, concat_axis=1, tiled=True)
    square_sum = jnp.sum(arrived[0, :, flat_piece:flat_piece + 3].astype(F32))
    clip_scale = 1.0 / jnp.maximum(1.0, jnp.sqrt(square_sum / (block_count * flat_piece * devices)))
    grad = arrived[:, :, :flat_piece].reshape(slot_count, block_width, block_width)
    slot_live = jnp.any(
        (owner_device[None, :] == my_index)
        & (state_slot[None, :] == jnp.arange(slot_count, dtype=jnp.int32)[:, None]),
        axis=1,
    )
    keeper = slot_live[:, None, None]

    scaled = grad.astype(F32) * clip_scale
    new_moment = average_decay * moment + (1.0 - average_decay) * scaled
    rotated = dot(dot(flipped(left_basis), scaled), right_basis)
    projected = dot(dot(flipped(left_basis), moment), right_basis)
    rotated_moment = average_decay * projected + (1.0 - average_decay) * rotated
    new_second = average_decay * second_moment + (1.0 - average_decay) * rotated * rotated
    ratio = rotated_moment / (jnp.sqrt(new_second) + stability)
    step_out = dot(dot(left_basis, ratio), flipped(right_basis))
    steps_out = jnp.where(keeper, step_out, 0.0)
    backward = lax.all_to_all(
        steps_out.reshape(slot_count, devices, flat_piece),
        ("dp", "mp"),
        split_axis=1,
        concat_axis=1,
        tiled=True,
    )
    direction = jnp.take(backward.reshape(slot_count * devices, flat_piece), slot_code, axis=0)

    weight = (1.0 - average_decay) / block_width * clip_scale * clip_scale
    new_left = average_decay * left_stat + weight * jnp.einsum(
        "sij,skj->sik", grad, grad, preferred_element_type=F32
    )
    new_right = average_decay * right_stat + weight * jnp.einsum(
        "sji,sjk->sik", grad, grad, preferred_element_type=F32
    )
    bases = refresh(
        jnp.concatenate([new_left, new_right], axis=0),
        jnp.concatenate([left_basis, right_basis], axis=0),
    )
    return (
        jnp.where(keeper, new_left, left_stat),
        jnp.where(keeper, new_right, right_stat),
        jnp.where(keeper, bases[:slot_count], left_basis),
        jnp.where(keeper, bases[slot_count:], right_basis),
        jnp.where(keeper, new_moment, moment),
        jnp.where(keeper, new_second, second_moment),
        direction,
    )


def solution(mesh):
    spread = P(("dp", "mp"), None, None)
    flat = P(None, ("dp", "mp"))
    return jax.shard_map(
        shards,
        mesh=mesh,
        in_specs=(flat, P(), P()) + (spread,) * 6,
        out_specs=(spread,) * 6 + (flat,),
        check_vma=False,
    )
```

```python
import functools

import jax
import jax.numpy as jnp
from jax import lax
from jax.experimental import pallas as pl
from jax.experimental.pallas import tpu as pltpu
from jax.sharding import PartitionSpec as P

N = 512
D = 128
LB = 32
PIECE = 2048
F32 = jnp.float32
BF16 = jnp.bfloat16
KEEP = 0.9
MIX = 1.0 - KEEP
STABILITY = 1e-08


def split(x):
    hi = x.astype(BF16)
    lo = (x - hi.astype(F32)).astype(BF16)
    return hi, lo


def dot3(a, b, ca, cb):
    dims = (((ca,), (cb,)), ((), ()))
    d = lambda x, y: lax.dot_general(x, y, dims, preferred_element_type=F32)
    return d(a[0], b[0]) + (d(a[0], b[1]) + d(a[1], b[0]))


def finish(ws, s, lb):
    lanes = lax.broadcasted_iota(jnp.int32, (lb, D), 1)
    on = lanes == lax.broadcasted_iota(jnp.int32, (lb, D), 0) + s * lb
    out = []
    for d, e in ws:
        piv = jnp.sum(jnp.where(on, d, 0.0), axis=1, keepdims=True)
        r = lax.rsqrt(piv)
        out.append((d * r, e * r))
    return out


def leaf(ws, s, lb):
    n = len(ws)
    sub = lax.broadcasted_iota(jnp.int32, (8, D), 0)
    ng = lb // 8
    ws = [([d[8 * i:8 * i + 8] for i in range(ng)], [e[8 * i:8 * i + 8] for i in range(ng)]) for d, e in ws]
    for g in range(ng):
        bc = []
        for b in range(n):
            ds, es = ws[b]
            bc.append([[jnp.broadcast_to(ds[i][:, s * lb + 8 * g + j:s * lb + 8 * g + j + 1], (8, D)) for i in range(g, ng)] for j in range(8)])
        for k in range(8):
            for b in range(n):
                ds, es = ws[b]
                cols = bc[b]
                own = cols[k]
                rp = 1.0 / jnp.broadcast_to(own[0][k:k + 1, :], (8, D))
                m = [x * rp for x in own]
                m[0] = jnp.where(sub > k, m[0], 0.0)
                for j in range(k + 1, 8):
                    w = jnp.broadcast_to(own[0][j:j + 1, :], (8, D))
                    cols[j] = [x - y * w for x, y in zip(cols[j], m)]
                rd = jnp.broadcast_to(ds[g][k:k + 1, :], (8, D))
                re = jnp.broadcast_to(es[g][k:k + 1, :], (8, D))
                for i in range(g, ng):
                    if i == g and k == 7:
                        continue
                    ds[i] = ds[i] - m[i - g] * rd
                    es[i] = es[i] - m[i - g] * re
    ws = [(jnp.concatenate(ds, axis=0), jnp.concatenate(es, axis=0)) for ds, es in ws]
    return finish(ws, s, lb)


def factor_body(nm, lb, a_ref, p_ref, q_ref, w_d, w_e):
    eye = (lax.broadcasted_iota(jnp.int32, (D, D), 0) == lax.broadcasted_iota(jnp.int32, (D, D), 1)).astype(F32)

    def step(k, carry):
        at = pl.ds(pl.multiple_of(k * D, D), D)
        for b in range(nm):
            w_d[b] = a_ref[b, at, at]
            w_e[b] = eye
        for s in range(D // lb):
            here = slice(s * lb, (s + 1) * lb)
            ws = [(w_d[b, here, :], w_e[b, here, :]) for b in range(nm)]
            ws = leaf(ws, s, lb)
            for b in range(nm):
                rd, re = ws[b]
                w_e[b, here, :] = re
                if s < D // lb - 1:
                    low = slice((s + 1) * lb, D)
                    dh, dl = split(rd)
                    eh, el = split(re)
                    lhs = jnp.concatenate([dh, dh, dl], axis=0)
                    rhs_d = jnp.concatenate([dh, dl, dh], axis=0)
                    rhs_e = jnp.concatenate([eh, el, eh], axis=0)
                    dims = (((0,), (0,)), ((), ()))
                    ud = lax.dot_general(lhs, rhs_d, dims, preferred_element_type=F32)
                    ue = lax.dot_general(lhs, rhs_e, dims, preferred_element_type=F32)
                    w_d[b, low, :] = w_d[b, low, :] - ud[(s + 1) * lb:, :]
                    w_e[b, low, :] = w_e[b, low, :] - ue[(s + 1) * lb:, :]
        for kk in range(N // D):
            @pl.when(k == kk)
            def _():
                o = kk * D
                for b in range(nm):
                    x = split(w_e[b])
                    q = dot3(split(p_ref[b, :, o:o + D]), x, 1, 1)
                    q_ref[b, :, o:o + D] = q
                    if kk < N // D - 1:
                        r = split(dot3(x, split(a_ref[b, o:o + D, o + D:]), 1, 0))
                        a_ref[b, o + D:, o + D:] = a_ref[b, o + D:, o + D:] - dot3(r, r, 0, 0)
                        p_ref[b, :, o + D:] = p_ref[b, :, o + D:] - dot3(split(q), r, 1, 0)
        return carry

    lax.fori_loop(0, N // D, step, 0)


def dot2(a, b, ca, cb):
    dims = (((ca,), (cb,)), ((), ()))
    d = lambda x, y: lax.dot_general(x, y, dims, preferred_element_type=F32)
    return d(a, b[0]) + d(a, b[1])


def dot2l(a, b, ca, cb):
    dims = (((ca,), (cb,)), ((), ()))
    d = lambda x, y: lax.dot_general(x, y, dims, preferred_element_type=F32)
    return d(a[0], b) + d(a[1], b)


def ahead_kernel(ls, rs, lb, rb, m, pl_out, pr_out, m2_out):
    l, r = split(lb[0]), split(rb[0])
    pl_out[0] = KEEP * dot3(split(ls[0]), l, 1, 0)
    pr_out[0] = KEEP * dot3(split(rs[0]), r, 1, 0)
    m2_out[0] = dot3(split(dot3(l, split(m[0]), 0, 0)), r, 1, 0)


def ahead(left_stat, right_stat, left_basis, right_basis, moment):
    one = pl.BlockSpec((1, N, N), lambda s: (s, 0, 0))
    return pl.pallas_call(
        ahead_kernel,
        grid=(2,),
        out_shape=[jax.ShapeDtypeStruct((2, N, N), F32)] * 3,
        in_specs=[one] * 5,
        out_specs=[one] * 3,
        compiler_params=pltpu.CompilerParams(vmem_limit_bytes=56 << 20),
        cost_estimate=pl.CostEstimate(flops=24 * 2 * N**3, bytes_accessed=16 * N * N * 4, transcendentals=0),
        name="ahead",
    )(left_stat, right_stat, left_basis, right_basis, moment)


def rotate_kernel(live, arr, lb, rb, m2, second, g_out, t_out, u_out, second_out, step_out, clip_out, x_s):
    s = pl.program_id(0)
    alive = live[s] > 0
    lanes = lax.broadcasted_iota(jnp.int32, (D, D), 1)
    terms = jnp.where(lanes < 3, arr[0, :, PIECE:].astype(F32), 0.0)
    total = jnp.sum(jnp.sum(terms, axis=1, keepdims=True), axis=0, keepdims=True)
    mean = total / (80.0 * N * N)
    clip = 1.0 / jnp.maximum(1.0, jnp.sqrt(mean))
    clip_out[...] = jnp.broadcast_to(clip, (8, D))
    for q in range(4):
        for c in range(4):
            x_s[c, pl.ds(q, D, stride=4), :] = arr[0, :, q * N + c * D:q * N + (c + 1) * D].astype(F32)
    g = jnp.concatenate([x_s[c] for c in range(4)], axis=1).astype(BF16)
    g_out[0] = g
    l, r = split(lb[0]), split(rb[0])
    t = dot2l(l, g, 0, 0)
    t_out[0] = t
    u_out[0] = dot2(g, r, 1, 0)
    rot = clip * dot3(split(t), r, 1, 0)
    v = KEEP * second[0] + MIX * rot * rot
    second_out[0] = jnp.where(alive, v, second[0])
    ratio = (KEEP * m2[0] + MIX * rot) / (jnp.sqrt(v) + STABILITY)
    step = dot3(split(dot3(l, split(ratio), 1, 0)), r, 1, 1)
    step = jnp.where(alive, step, 0.0)
    for c in range(4):
        x_s[c] = step[:, c * D:(c + 1) * D]
        for q in range(4):
            step_out[0, :, q * N + c * D:q * N + (c + 1) * D] = x_s[c, pl.ds(q, D, stride=4), :]


def rotate(live, arrived, left_basis, right_basis, m2, second):
    one = pl.BlockSpec((1, N, N), lambda s: (s, 0, 0))
    width = arrived.shape[-1]
    return pl.pallas_call(
        rotate_kernel,
        grid=(2,),
        out_shape=[
            jax.ShapeDtypeStruct((2, N, N), BF16),
            jax.ShapeDtypeStruct((2, N, N), F32),
            jax.ShapeDtypeStruct((2, N, N), F32),
            jax.ShapeDtypeStruct((2, N, N), F32),
            jax.ShapeDtypeStruct((2, D, PIECE), F32),
            jax.ShapeDtypeStruct((8, D), F32),
        ],
        in_specs=[
            pl.BlockSpec(memory_space=pltpu.SMEM),
            pl.BlockSpec((1, D, width), lambda s: (s, 0, 0)),
            one, one, one, one,
        ],
        out_specs=[one] * 4 + [
            pl.BlockSpec((1, D, PIECE), lambda s: (s, 0, 0)),
            pl.BlockSpec((8, D), lambda s: (0, 0)),
        ],
        scratch_shapes=[pltpu.VMEM((4, N, D), F32)],
        compiler_params=pltpu.CompilerParams(vmem_limit_bytes=56 << 20),
        cost_estimate=pl.CostEstimate(flops=30 * 2 * N**3, bytes_accessed=20 * N * N * 4, transcendentals=0),
        name="rotate",
    )(live, arrived, left_basis, right_basis, m2, second)


def refresh_kernel(live, clip_ref, g_ref, t_ref, u_ref, pl_ref, pr_ref, ls_h, rs_h, lb_h, rb_h, m_h,
                   nls_h, nrs_h, nlb_h, nrb_h, nm_h,
                   a_ref, p_ref, q_ref, w_d, w_e, st, bs, mo, in_sem, out_sem):
    ins = [(ls_h, st.at[pl.ds(0, 2)]), (rs_h, st.at[pl.ds(2, 2)]), (m_h, mo), (lb_h, bs.at[pl.ds(0, 2)]), (rb_h, bs.at[pl.ds(2, 2)])]
    loads = [pltpu.make_async_copy(src, dst, in_sem.at[i]) for i, (src, dst) in enumerate(ins)]
    for c in loads:
        c.start()
    clip = clip_ref[0:1, 0:1]
    weight = (MIX / N) * clip * clip
    for s in range(2):
        g = g_ref[s]
        p = pl_ref[s] + weight * dot2(g, split(t_ref[s]), 1, 1)
        p_ref[s] = p
        p = split(p)
        a_ref[s] = dot3(p, p, 0, 0)
        p = pr_ref[s] + weight * dot2(g, split(u_ref[s]), 0, 0)
        p_ref[2 + s] = p
        p = split(p)
        a_ref[2 + s] = dot3(p, p, 0, 0)
    for c in loads[:3]:
        c.wait()
    for s in range(2):
        alive = live[s] > 0
        g = g_ref[s]
        one = lambda c: lax.dot_general(g, g, (((c,), (c,)), ((), ())), preferred_element_type=F32)
        st[s] = jnp.where(alive, KEEP * st[s] + weight * one(1), st[s])
        st[2 + s] = jnp.where(alive, KEEP * st[2 + s] + weight * one(0), st[2 + s])
        mo[s] = jnp.where(alive, KEEP * mo[s] + (MIX * clip) * g.astype(F32), mo[s])
    outs = [(st.at[pl.ds(0, 2)], nls_h), (st.at[pl.ds(2, 2)], nrs_h), (mo, nm_h)]
    stores = [pltpu.make_async_copy(src, dst, out_sem.at[i]) for i, (src, dst) in enumerate(outs)]
    for c in stores:
        c.start()
    factor_body(4, LB, a_ref, p_ref, q_ref, w_d, w_e)
    for c in loads[3:]:
        c.wait()
    for s in range(2):
        alive = live[s] > 0
        q_ref[s] = jnp.where(alive, q_ref[s], bs[s])
        q_ref[2 + s] = jnp.where(alive, q_ref[2 + s], bs[2 + s])
    outs = [(q_ref.at[pl.ds(0, 2)], nlb_h), (q_ref.at[pl.ds(2, 2)], nrb_h)]
    last = [pltpu.make_async_copy(src, dst, out_sem.at[3 + i]) for i, (src, dst) in enumerate(outs)]
    for c in last:
        c.start()
    for c in stores + last:
        c.wait()


def refresh(live, clip, g, t, u, p_left, p_right, left_stat, right_stat, left_basis, right_basis, moment):
    vm = pl.BlockSpec(memory_space=pltpu.VMEM)
    hb = pl.BlockSpec(memory_space=pl.ANY)
    return pl.pallas_call(
        refresh_kernel,
        out_shape=[jax.ShapeDtypeStruct((2, N, N), F32)] * 5,
        in_specs=[pl.BlockSpec(memory_space=pltpu.SMEM)] + [vm] * 6 + [hb] * 5,
        out_specs=[hb] * 5,
        scratch_shapes=[
            pltpu.VMEM((4, N, N), F32),
            pltpu.VMEM((4, N, N), F32),
            pltpu.VMEM((4, N, N), F32),
            pltpu.VMEM((4, D, D), F32),
            pltpu.VMEM((4, D, D), F32),
            pltpu.VMEM((4, N, N), F32),
            pltpu.VMEM((4, N, N), F32),
            pltpu.VMEM((2, N, N), F32),
            pltpu.SemaphoreType.DMA((5,)),
            pltpu.SemaphoreType.DMA((5,)),
        ],
        compiler_params=pltpu.CompilerParams(vmem_limit_bytes=56 << 20),
        cost_estimate=pl.CostEstimate(flops=100 * 2 * N**3, bytes_accessed=30 * N * N * 4, transcendentals=0),
        name="refresh",
    )(live, clip, g, t, u, p_left, p_right, left_stat, right_stat, left_basis, right_basis, moment)


def shards(
    gradient,
    owner_device,
    state_slot,
    left_stat,
    right_stat,
    left_basis,
    right_basis,
    moment,
    second_moment,
):
    devices = lax.axis_size(("dp", "mp"))
    slot_count = left_stat.shape[0]
    flat_piece = gradient.shape[1]
    my_index = lax.axis_index(("dp", "mp"))
    own_square = jnp.sum(jnp.square(gradient.astype(F32)))
    first = own_square.astype(BF16)
    second = (own_square - first.astype(F32)).astype(BF16)
    third = (own_square - first.astype(F32) - second.astype(F32)).astype(BF16)
    terms = jnp.stack([first, second, third])
    slot_code = state_slot * devices + owner_device
    picker = (
        slot_code[None, :] == jnp.arange(slot_count * devices, dtype=jnp.int32)[:, None]
    ).astype(BF16)
    outgoing = jnp.dot(picker, gradient, preferred_element_type=F32).astype(BF16)
    outgoing = outgoing.reshape(slot_count, devices, flat_piece)
    tail = jnp.broadcast_to(jnp.pad(terms, (0, 125)), (slot_count, devices, 128))
    outgoing = jnp.concatenate([outgoing, tail], axis=2)
    arrived = lax.all_to_all(outgoing, ("dp", "mp"), split_axis=1, concat_axis=1, tiled=True)
    p_left, p_right, rotated_old = ahead(left_stat, right_stat, left_basis, right_basis, moment)
    live = jnp.any(
        (owner_device[None, :] == my_index)
        & (state_slot[None, :] == jnp.arange(slot_count, dtype=jnp.int32)[:, None]),
        axis=1,
    ).astype(jnp.int32)
    g, t, u, new_second, steps, clip = rotate(
        live, arrived, left_basis, right_basis, rotated_old, second_moment
    )
    backward = lax.all_to_all(steps, ("dp", "mp"), split_axis=1, concat_axis=1, tiled=True)
    new_left, new_right, new_left_basis, new_right_basis, new_moment = refresh(
        live, clip, g, t, u, p_left, p_right, left_stat, right_stat, left_basis, right_basis, moment
    )
    direction = jnp.take(backward.reshape(slot_count * devices, flat_piece), slot_code, axis=0)
    return (
        new_left,
        new_right,
        new_left_basis,
        new_right_basis,
        new_moment,
        new_second,
        direction,
    )


def solution(mesh):
    spread = P(("dp", "mp"), None, None)
    flat = P(None, ("dp", "mp"))
    return jax.shard_map(
        shards,
        mesh=mesh,
        in_specs=(flat, P(), P()) + (spread,) * 6,
        out_specs=(spread,) * 6 + (flat,),
        check_vma=False,
    )
```

```python
import functools

import jax
import jax.numpy as jnp
from jax import lax
from jax.experimental import pallas as pl
from jax.experimental.pallas import tpu as pltpu
from jax.sharding import PartitionSpec as P

N = 512
D = 128
LB = 32
PIECE = 2048
F32 = jnp.float32
BF16 = jnp.bfloat16
KEEP = 0.9
MIX = 1.0 - KEEP
STABILITY = 1e-08


def split(x):
    hi = x.astype(BF16)
    lo = (x - hi.astype(F32)).astype(BF16)
    return hi, lo


def dot3(a, b, ca, cb):
    dims = (((ca,), (cb,)), ((), ()))
    d = lambda x, y: lax.dot_general(x, y, dims, preferred_element_type=F32)
    return d(a[0], b[0]) + (d(a[0], b[1]) + d(a[1], b[0]))


def finish(ws, s, lb):
    lanes = lax.broadcasted_iota(jnp.int32, (lb, D), 1)
    on = lanes == lax.broadcasted_iota(jnp.int32, (lb, D), 0) + s * lb
    out = []
    for d, e in ws:
        piv = jnp.sum(jnp.where(on, d, 0.0), axis=1, keepdims=True)
        r = lax.rsqrt(piv)
        out.append((d * r, e * r))
    return out


def leaf(ws, s, lb):
    n = len(ws)
    sub = lax.broadcasted_iota(jnp.int32, (8, D), 0)
    ng = lb // 8
    ws = [([d[8 * i:8 * i + 8] for i in range(ng)], [e[8 * i:8 * i + 8] for i in range(ng)]) for d, e in ws]
    for g in range(ng):
        bc = []
        for b in range(n):
            ds, es = ws[b]
            bc.append([[jnp.broadcast_to(ds[i][:, s * lb + 8 * g + j:s * lb + 8 * g + j + 1], (8, D)) for i in range(g, ng)] for j in range(8)])
        for k in range(8):
            for b in range(n):
                ds, es = ws[b]
                cols = bc[b]
                own = cols[k]
                rp = 1.0 / jnp.broadcast_to(own[0][k:k + 1, :], (8, D))
                m = [x * rp for x in own]
                m[0] = jnp.where(sub > k, m[0], 0.0)
                for j in range(k + 1, 8):
                    w = jnp.broadcast_to(own[0][j:j + 1, :], (8, D))
                    cols[j] = [x - y * w for x, y in zip(cols[j], m)]
                rd = jnp.broadcast_to(ds[g][k:k + 1, :], (8, D))
                re = jnp.broadcast_to(es[g][k:k + 1, :], (8, D))
                for i in range(g, ng):
                    if i == g and k == 7:
                        continue
                    ds[i] = ds[i] - m[i - g] * rd
                    es[i] = es[i] - m[i - g] * re
    ws = [(jnp.concatenate(ds, axis=0), jnp.concatenate(es, axis=0)) for ds, es in ws]
    return finish(ws, s, lb)


def factor_body(nm, lb, a_ref, p_ref, q_ref, w_d, w_e):
    eye = (lax.broadcasted_iota(jnp.int32, (D, D), 0) == lax.broadcasted_iota(jnp.int32, (D, D), 1)).astype(F32)

    def step(k, carry):
        at = pl.ds(pl.multiple_of(k * D, D), D)
        for b in range(nm):
            w_d[b] = a_ref[b, at, at]
            w_e[b] = eye
        for s in range(D // lb):
            here = slice(s * lb, (s + 1) * lb)
            ws = [(w_d[b, here, :], w_e[b, here, :]) for b in range(nm)]
            ws = leaf(ws, s, lb)
            for b in range(nm):
                rd, re = ws[b]
                w_e[b, here, :] = re
                if s < D // lb - 1:
                    low = slice((s + 1) * lb, D)
                    dh, dl = split(rd)
                    eh, el = split(re)
                    lhs = jnp.concatenate([dh, dh, dl], axis=0)
                    rhs_d = jnp.concatenate([dh, dl, dh], axis=0)
                    rhs_e = jnp.concatenate([eh, el, eh], axis=0)
                    dims = (((0,), (0,)), ((), ()))
                    ud = lax.dot_general(lhs, rhs_d, dims, preferred_element_type=F32)
                    ue = lax.dot_general(lhs, rhs_e, dims, preferred_element_type=F32)
                    w_d[b, low, :] = w_d[b, low, :] - ud[(s + 1) * lb:, :]
                    w_e[b, low, :] = w_e[b, low, :] - ue[(s + 1) * lb:, :]
        for kk in range(N // D):
            @pl.when(k == kk)
            def _():
                o = kk * D
                for b in range(nm):
                    x = split(w_e[b])
                    q = dot3(split(p_ref[b, :, o:o + D]), x, 1, 1)
                    q_ref[b, :, o:o + D] = q
                    if kk < N // D - 1:
                        r = split(dot3(x, split(a_ref[b, o:o + D, o + D:]), 1, 0))
                        a_ref[b, o + D:, o + D:] = a_ref[b, o + D:, o + D:] - dot3(r, r, 0, 0)
                        p_ref[b, :, o + D:] = p_ref[b, :, o + D:] - dot3(split(q), r, 1, 0)
        return carry

    lax.fori_loop(0, N // D, step, 0)


def dot2(a, b, ca, cb):
    dims = (((ca,), (cb,)), ((), ()))
    d = lambda x, y: lax.dot_general(x, y, dims, preferred_element_type=F32)
    return d(a, b[0]) + d(a, b[1])


def dot2l(a, b, ca, cb):
    dims = (((ca,), (cb,)), ((), ()))
    d = lambda x, y: lax.dot_general(x, y, dims, preferred_element_type=F32)
    return d(a[0], b) + d(a[1], b)


def ahead_kernel(devices, mp, code, grad, ls_h, rs_h, lb_h, rb_h, m_h, pl_h, pr_h, m2_h, g_out, clip_out,
                 stage, away, arr, x_s, st, bs, mo, res, in_sem, out_sem, send_sem, recv_sem):
    me = lax.axis_index("dp") * mp + lax.axis_index("mp")
    place = lambda d: {"dp": lax.div(d, mp), "mp": lax.rem(d, mp)}
    barrier = pltpu.get_barrier_semaphore()

    def greet(i, carry):
        pl.semaphore_signal(barrier, inc=1, device_id=place(lax.rem(me + i, devices)), device_id_type=pl.DeviceIdType.MESH)
        return carry

    lax.fori_loop(1, devices, greet, 0)
    ins = [(lb_h, bs.at[pl.ds(0, 2)]), (ls_h, st.at[pl.ds(0, 2)]), (rb_h, bs.at[pl.ds(2, 2)]), (rs_h, st.at[pl.ds(2, 2)]), (m_h, mo)]
    loads = [pltpu.make_async_copy(src, dst, in_sem.at[n]) for n, (src, dst) in enumerate(ins)]
    for c in loads:
        c.start()

    g = grad[...]
    gf = g.astype(F32)
    own = jnp.sum(jnp.sum(gf * gf, axis=1, keepdims=True), axis=0, keepdims=True)
    first = own.astype(BF16).astype(F32)
    second = (own - first).astype(BF16).astype(F32)
    third = own - first - second
    rows = lax.broadcasted_iota(jnp.int32, (16, D), 0)
    tile = jnp.where(rows == 0, first, jnp.where(rows == 1, second, jnp.where(rows == 2, third, 0.0))).astype(BF16)
    for s in range(2):
        names = lax.broadcasted_iota(jnp.int32, (devices, code.shape[1]), 0) + s * devices
        picker = (names == code[...]).astype(BF16)
        row = jnp.dot(picker, g, preferred_element_type=F32)
        for r in range(16):
            stage[s, pl.ds(r, devices, stride=16), :] = row[:, r * D:(r + 1) * D]
        away[:, 16 * s:16 * s + 16, :] = stage[s].astype(BF16).reshape(devices, 16, D)
    away[:, 32:48, :] = jnp.broadcast_to(tile, (devices, 16, D))
    pl.semaphore_wait(barrier, devices - 1)

    def send(i, carry):
        to = lax.rem(me + i, devices)
        pltpu.make_async_remote_copy(
            src_ref=away.at[to], dst_ref=arr.at[me], send_sem=send_sem, recv_sem=recv_sem,
            device_id=place(to), device_id_type=pl.DeviceIdType.MESH,
        ).start()
        return carry

    lax.fori_loop(1, devices, send, 0)
    keep = pltpu.make_async_copy(away.at[me], arr.at[me], in_sem.at[5])
    keep.start()

    loads[0].wait()
    loads[1].wait()
    for s in range(2):
        res[s] = KEEP * dot3(split(st[s]), split(bs[s]), 1, 0)
    outs = [pltpu.make_async_copy(res.at[pl.ds(0, 2)], pl_h, out_sem.at[0])]
    outs[0].start()
    loads[2].wait()
    loads[3].wait()
    for s in range(2):
        res[2 + s] = KEEP * dot3(split(st[2 + s]), split(bs[2 + s]), 1, 0)
    outs.append(pltpu.make_async_copy(res.at[pl.ds(2, 2)], pr_h, out_sem.at[1]))
    outs[1].start()
    loads[4].wait()
    for s in range(2):
        res[4 + s] = dot3(split(dot3(split(bs[s]), split(mo[s]), 0, 0)), split(bs[2 + s]), 1, 0)
    outs.append(pltpu.make_async_copy(res.at[pl.ds(4, 2)], m2_h, out_sem.at[2]))
    outs[2].start()
    keep.wait()
    most = arr.at[pl.ds(0, devices - 1)]
    pltpu.make_async_copy(most, most, recv_sem).wait()
    pltpu.make_async_copy(most, most, send_sem).wait()

    terms = arr[:, 32:48, :].astype(F32)
    total = jnp.sum(jnp.sum(terms, axis=0), axis=0, keepdims=True)
    mean = total / (80.0 * N * N)
    clip_out[...] = jnp.broadcast_to(1.0 / jnp.maximum(1.0, jnp.sqrt(mean)), (8, D))
    for s in range(2):
        stage[s] = arr[:, 16 * s:16 * s + 16, :].astype(F32).reshape(16 * devices, D)
        for q in range(4):
            for c in range(4):
                x_s[c, pl.ds(q, D, stride=4), :] = stage[s, pl.ds(4 * q + c, devices, stride=16), :]
        for c in range(4):
            g_out[s, :, c * D:(c + 1) * D] = x_s[c].astype(BF16)
    for c in outs:
        c.wait()


def ahead(code, gradient, left_stat, right_stat, left_basis, right_basis, moment):
    devices, mp = lax.axis_size(("dp", "mp")), lax.axis_size("mp")
    vm = pl.BlockSpec(memory_space=pltpu.VMEM)
    hb = pl.BlockSpec(memory_space=pl.ANY)
    return pl.pallas_call(
        functools.partial(ahead_kernel, devices, mp),
        out_shape=[jax.ShapeDtypeStruct((2, N, N), F32)] * 3
        + [jax.ShapeDtypeStruct((2, N, N), BF16), jax.ShapeDtypeStruct((8, D), F32)],
        in_specs=[vm, vm] + [hb] * 5,
        out_specs=[hb] * 3 + [vm, vm],
        scratch_shapes=[
            pltpu.VMEM((2, 16 * devices, D), F32),
            pltpu.VMEM((devices, 48, D), BF16),
            pltpu.VMEM((devices, 48, D), BF16),
            pltpu.VMEM((4, N, D), F32),
            pltpu.VMEM((4, N, N), F32),
            pltpu.VMEM((4, N, N), F32),
            pltpu.VMEM((2, N, N), F32),
            pltpu.VMEM((6, N, N), F32),
            pltpu.SemaphoreType.DMA((6,)),
            pltpu.SemaphoreType.DMA((3,)),
            pltpu.SemaphoreType.DMA,
            pltpu.SemaphoreType.DMA,
        ],
        compiler_params=pltpu.CompilerParams(
            vmem_limit_bytes=56 << 20, collective_id=0, has_side_effects=True
        ),
        cost_estimate=pl.CostEstimate(flops=24 * 2 * N**3, bytes_accessed=16 * N * N * 4, transcendentals=0),
        name="ahead",
    )(code, gradient, left_stat, right_stat, left_basis, right_basis, moment)


def rotate_kernel(live, clip_in, g_in, lb, rb, m2, second, t_out, u_out, second_out, step_out, x_s):
    s = pl.program_id(0)
    alive = live[s] > 0
    g = g_in[0]
    clip = clip_in[0:1, 0:1]
    l, r = split(lb[0]), split(rb[0])
    t = dot2l(l, g, 0, 0)
    t_out[0] = t
    u_out[0] = dot2(g, r, 1, 0)
    rot = clip * dot3(split(t), r, 1, 0)
    v = KEEP * second[0] + MIX * rot * rot
    second_out[0] = jnp.where(alive, v, second[0])
    ratio = (KEEP * m2[0] + MIX * rot) / (jnp.sqrt(v) + STABILITY)
    step = dot3(split(dot3(l, split(ratio), 1, 0)), r, 1, 1)
    step = jnp.where(alive, step, 0.0)
    for c in range(4):
        x_s[c] = step[:, c * D:(c + 1) * D]
        for q in range(4):
            step_out[0, :, q * N + c * D:q * N + (c + 1) * D] = x_s[c, pl.ds(q, D, stride=4), :]


def rotate(live, clip, g, left_basis, right_basis, m2, second):
    one = pl.BlockSpec((1, N, N), lambda s: (s, 0, 0))
    return pl.pallas_call(
        rotate_kernel,
        grid=(2,),
        out_shape=[
            jax.ShapeDtypeStruct((2, N, N), F32),
            jax.ShapeDtypeStruct((2, N, N), F32),
            jax.ShapeDtypeStruct((2, N, N), F32),
            jax.ShapeDtypeStruct((2, D, PIECE), F32),
        ],
        in_specs=[
            pl.BlockSpec(memory_space=pltpu.SMEM),
            pl.BlockSpec((8, D), lambda s: (0, 0)),
            one, one, one, one, one,
        ],
        out_specs=[one] * 3 + [pl.BlockSpec((1, D, PIECE), lambda s: (s, 0, 0))],
        scratch_shapes=[pltpu.VMEM((4, N, D), F32)],
        compiler_params=pltpu.CompilerParams(vmem_limit_bytes=56 << 20),
        cost_estimate=pl.CostEstimate(flops=30 * 2 * N**3, bytes_accessed=20 * N * N * 4, transcendentals=0),
        name="rotate",
    )(live, clip, g, left_basis, right_basis, m2, second)


def refresh_kernel(live, clip_ref, g_ref, t_ref, u_ref, pl_ref, pr_ref, ls_h, rs_h, lb_h, rb_h, m_h,
                   nls_h, nrs_h, nlb_h, nrb_h, nm_h,
                   a_ref, p_ref, q_ref, w_d, w_e, st, bs, mo, in_sem, out_sem):
    ins = [(ls_h, st.at[pl.ds(0, 2)]), (rs_h, st.at[pl.ds(2, 2)]), (m_h, mo), (lb_h, bs.at[pl.ds(0, 2)]), (rb_h, bs.at[pl.ds(2, 2)])]
    loads = [pltpu.make_async_copy(src, dst, in_sem.at[i]) for i, (src, dst) in enumerate(ins)]
    for c in loads:
        c.start()
    clip = clip_ref[0:1, 0:1]
    weight = (MIX / N) * clip * clip
    for s in range(2):
        g = g_ref[s]
        p = pl_ref[s] + weight * dot2(g, split(t_ref[s]), 1, 1)
        p_ref[s] = p
        p = split(p)
        a_ref[s] = dot3(p, p, 0, 0)
        p = pr_ref[s] + weight * dot2(g, split(u_ref[s]), 0, 0)
        p_ref[2 + s] = p
        p = split(p)
        a_ref[2 + s] = dot3(p, p, 0, 0)
    for c in loads[:3]:
        c.wait()
    for s in range(2):
        alive = live[s] > 0
        g = g_ref[s]
        one = lambda c: lax.dot_general(g, g, (((c,), (c,)), ((), ())), preferred_element_type=F32)
        st[s] = jnp.where(alive, KEEP * st[s] + weight * one(1), st[s])
        st[2 + s] = jnp.where(alive, KEEP * st[2 + s] + weight * one(0), st[2 + s])
        mo[s] = jnp.where(alive, KEEP * mo[s] + (MIX * clip) * g.astype(F32), mo[s])
    outs = [(st.at[pl.ds(0, 2)], nls_h), (st.at[pl.ds(2, 2)], nrs_h), (mo, nm_h)]
    stores = [pltpu.make_async_copy(src, dst, out_sem.at[i]) for i, (src, dst) in enumerate(outs)]
    for c in stores:
        c.start()
    factor_body(4, LB, a_ref, p_ref, q_ref, w_d, w_e)
    for c in loads[3:]:
        c.wait()
    for s in range(2):
        alive = live[s] > 0
        q_ref[s] = jnp.where(alive, q_ref[s], bs[s])
        q_ref[2 + s] = jnp.where(alive, q_ref[2 + s], bs[2 + s])
    outs = [(q_ref.at[pl.ds(0, 2)], nlb_h), (q_ref.at[pl.ds(2, 2)], nrb_h)]
    last = [pltpu.make_async_copy(src, dst, out_sem.at[3 + i]) for i, (src, dst) in enumerate(outs)]
    for c in last:
        c.start()
    for c in stores + last:
        c.wait()


def refresh(live, clip, g, t, u, p_left, p_right, left_stat, right_stat, left_basis, right_basis, moment):
    vm = pl.BlockSpec(memory_space=pltpu.VMEM)
    hb = pl.BlockSpec(memory_space=pl.ANY)
    return pl.pallas_call(
        refresh_kernel,
        out_shape=[jax.ShapeDtypeStruct((2, N, N), F32)] * 5,
        in_specs=[pl.BlockSpec(memory_space=pltpu.SMEM)] + [vm] * 6 + [hb] * 5,
        out_specs=[hb] * 5,
        scratch_shapes=[
            pltpu.VMEM((4, N, N), F32),
            pltpu.VMEM((4, N, N), F32),
            pltpu.VMEM((4, N, N), F32),
            pltpu.VMEM((4, D, D), F32),
            pltpu.VMEM((4, D, D), F32),
            pltpu.VMEM((4, N, N), F32),
            pltpu.VMEM((4, N, N), F32),
            pltpu.VMEM((2, N, N), F32),
            pltpu.SemaphoreType.DMA((5,)),
            pltpu.SemaphoreType.DMA((5,)),
        ],
        compiler_params=pltpu.CompilerParams(vmem_limit_bytes=56 << 20),
        cost_estimate=pl.CostEstimate(flops=100 * 2 * N**3, bytes_accessed=30 * N * N * 4, transcendentals=0),
        name="refresh",
    )(live, clip, g, t, u, p_left, p_right, left_stat, right_stat, left_basis, right_basis, moment)


def shards(
    gradient,
    owner_device,
    state_slot,
    left_stat,
    right_stat,
    left_basis,
    right_basis,
    moment,
    second_moment,
):
    devices = lax.axis_size(("dp", "mp"))
    slot_count = left_stat.shape[0]
    flat_piece = gradient.shape[1]
    my_index = lax.axis_index(("dp", "mp"))
    slot_code = state_slot * devices + owner_device
    p_left, p_right, rotated_old, g, clip = ahead(
        slot_code[None, :], gradient, left_stat, right_stat, left_basis, right_basis, moment
    )
    live = jnp.any(
        (owner_device[None, :] == my_index)
        & (state_slot[None, :] == jnp.arange(slot_count, dtype=jnp.int32)[:, None]),
        axis=1,
    ).astype(jnp.int32)
    t, u, new_second, steps = rotate(
        live, clip, g, left_basis, right_basis, rotated_old, second_moment
    )
    backward = lax.all_to_all(steps, ("dp", "mp"), split_axis=1, concat_axis=1, tiled=True)
    new_left, new_right, new_left_basis, new_right_basis, new_moment = refresh(
        live, clip, g, t, u, p_left, p_right, left_stat, right_stat, left_basis, right_basis, moment
    )
    direction = jnp.take(backward.reshape(slot_count * devices, flat_piece), slot_code, axis=0)
    return (
        new_left,
        new_right,
        new_left_basis,
        new_right_basis,
        new_moment,
        new_second,
        direction,
    )


def solution(mesh):
    spread = P(("dp", "mp"), None, None)
    flat = P(None, ("dp", "mp"))
    return jax.shard_map(
        shards,
        mesh=mesh,
        in_specs=(flat, P(), P()) + (spread,) * 6,
        out_specs=(spread,) * 6 + (flat,),
        check_vma=False,
    )
```

```python
import functools

import jax
import jax.numpy as jnp
from jax import lax
from jax.experimental import pallas as pl
from jax.experimental.pallas import tpu as pltpu
from jax.sharding import PartitionSpec as P

N = 512
D = 128
LB = 32
PIECE = 2048
F32 = jnp.float32
BF16 = jnp.bfloat16
KEEP = 0.9
MIX = 1.0 - KEEP
STABILITY = 1e-08


def split(x):
    hi = x.astype(BF16)
    lo = (x - hi.astype(F32)).astype(BF16)
    return hi, lo


def dot3(a, b, ca, cb):
    dims = (((ca,), (cb,)), ((), ()))
    d = lambda x, y: lax.dot_general(x, y, dims, preferred_element_type=F32)
    return d(a[0], b[0]) + (d(a[0], b[1]) + d(a[1], b[0]))


def finish(ws, s, lb):
    lanes = lax.broadcasted_iota(jnp.int32, (lb, D), 1)
    on = lanes == lax.broadcasted_iota(jnp.int32, (lb, D), 0) + s * lb
    out = []
    for d, e in ws:
        piv = jnp.sum(jnp.where(on, d, 0.0), axis=1, keepdims=True)
        r = lax.rsqrt(piv)
        out.append((d * r, e * r))
    return out


def leaf(ws, s, lb):
    n = len(ws)
    sub = lax.broadcasted_iota(jnp.int32, (8, D), 0)
    ng = lb // 8
    ws = [([d[8 * i:8 * i + 8] for i in range(ng)], [e[8 * i:8 * i + 8] for i in range(ng)]) for d, e in ws]
    for g in range(ng):
        bc = []
        for b in range(n):
            ds, es = ws[b]
            bc.append([[jnp.broadcast_to(ds[i][:, s * lb + 8 * g + j:s * lb + 8 * g + j + 1], (8, D)) for i in range(g, ng)] for j in range(8)])
        for k in range(8):
            for b in range(n):
                ds, es = ws[b]
                cols = bc[b]
                own = cols[k]
                rp = 1.0 / jnp.broadcast_to(own[0][k:k + 1, :], (8, D))
                m = [x * rp for x in own]
                m[0] = jnp.where(sub > k, m[0], 0.0)
                for j in range(k + 1, 8):
                    w = jnp.broadcast_to(own[0][j:j + 1, :], (8, D))
                    cols[j] = [x - y * w for x, y in zip(cols[j], m)]
                rd = jnp.broadcast_to(ds[g][k:k + 1, :], (8, D))
                re = jnp.broadcast_to(es[g][k:k + 1, :], (8, D))
                for i in range(g, ng):
                    if i == g and k == 7:
                        continue
                    ds[i] = ds[i] - m[i - g] * rd
                    es[i] = es[i] - m[i - g] * re
    ws = [(jnp.concatenate(ds, axis=0), jnp.concatenate(es, axis=0)) for ds, es in ws]
    return finish(ws, s, lb)


def dot2(a, b, ca, cb):
    dims = (((ca,), (cb,)), ((), ()))
    d = lambda x, y: lax.dot_general(x, y, dims, preferred_element_type=F32)
    return d(a, b[0]) + d(a, b[1])


def dot2l(a, b, ca, cb):
    dims = (((ca,), (cb,)), ((), ()))
    d = lambda x, y: lax.dot_general(x, y, dims, preferred_element_type=F32)
    return d(a[0], b) + d(a[1], b)


def travel_kernel(devices, mp, code, grad, ls_h, lb_h, rs_h, rb_h, m_h, v_h,
                  a_h, p_h, g_h, rot_h, step_h, clip_out,
                  stage, away, arr, sq, sqs, x_s, st, bs, mo, vs, g_s, ps, gram, rots, steps,
                  in_sem, out_sem, send_sem, recv_sem):
    me = lax.axis_index("dp") * mp + lax.axis_index("mp")
    place = lambda d: {"dp": lax.div(d, mp), "mp": lax.rem(d, mp)}
    barrier = pltpu.get_barrier_semaphore()

    def greet(i, carry):
        pl.semaphore_signal(barrier, inc=1, device_id=place(lax.rem(me + i, devices)), device_id_type=pl.DeviceIdType.MESH)
        return carry

    lax.fori_loop(1, devices, greet, 0)
    ins = [(lb_h, bs.at[pl.ds(0, 2)]), (ls_h, st.at[pl.ds(0, 2)]), (rb_h, bs.at[pl.ds(2, 2)]), (rs_h, st.at[pl.ds(2, 2)]), (m_h, mo), (v_h, vs)]
    loads = [pltpu.make_async_copy(src, dst, in_sem.at[n]) for n, (src, dst) in enumerate(ins)]
    for c in loads:
        c.start()

    g = grad[...]
    for s in range(2):
        names = lax.broadcasted_iota(jnp.int32, (devices, code.shape[1]), 0) + s * devices
        picker = (names == code[...]).astype(BF16)
        row = jnp.dot(picker, g, preferred_element_type=F32)
        for r in range(16):
            stage[s, pl.ds(r, devices, stride=16), :] = row[:, r * D:(r + 1) * D]
        away[s] = stage[s].astype(BF16).reshape(devices, 16, D)
    gf = g.astype(F32)
    own = jnp.sum(jnp.sum(gf * gf, axis=1, keepdims=True), axis=0, keepdims=True)
    sq[0] = jnp.broadcast_to(own, (1, D))
    sqs[me] = sq[0]
    pl.semaphore_wait(barrier, devices - 1)

    def send(src, dst, n):
        def one(i, carry):
            to = lax.rem(me + i, devices)
            pltpu.make_async_remote_copy(
                src_ref=src(to), dst_ref=dst, send_sem=send_sem.at[n], recv_sem=recv_sem.at[n],
                device_id=place(to), device_id_type=pl.DeviceIdType.MESH,
            ).start()
            return carry

        lax.fori_loop(1, devices, one, 0)

    send(lambda to: away.at[0, to], arr.at[0, me], 0)
    send(lambda to: sq.at[0], sqs.at[me], 2)
    send(lambda to: away.at[1, to], arr.at[1, me], 1)
    keep = [pltpu.make_async_copy(away.at[s, me], arr.at[s, me], in_sem.at[6 + s]) for s in range(2)]
    for c in keep:
        c.start()

    for c in loads[:4]:
        c.wait()
    for b in range(4):
        ps[b] = KEEP * dot3(split(st[b]), split(bs[b]), 1, 0)
    loads[4].wait()
    for s in range(2):
        rots[s] = dot3(split(dot3(split(bs[s]), split(mo[s]), 0, 0)), split(bs[2 + s]), 1, 0)
    loads[5].wait()
    most = pl.ds(0, devices - 1)
    outs = []

    def put(src, dst):
        outs.append(pltpu.make_async_copy(src, dst, out_sem.at[len(outs)]))
        outs[-1].start()

    for s in range(2):
        pltpu.make_async_copy(arr.at[s, most], arr.at[s, most], recv_sem.at[s]).wait()
        keep[s].wait()
        if s == 0:
            pltpu.make_async_copy(sqs.at[most], sqs.at[most], recv_sem.at[2]).wait()
            mean = jnp.sum(sqs[...], axis=0) / (80.0 * N * N)
            clips = 1.0 / jnp.maximum(1.0, jnp.sqrt(mean))
            clip_out[...] = jnp.broadcast_to(clips, (8, D))
            clip = clips[:, 0:1]
            weight = (MIX / N) * clip * clip
        stage[s] = arr[s].astype(F32).reshape(16 * devices, D)
        for q in range(4):
            for c in range(4):
                x_s[c, pl.ds(q, D, stride=4), :] = stage[s, pl.ds(4 * q + c, devices, stride=16), :]
        for c in range(4):
            g_s[s, :, c * D:(c + 1) * D] = x_s[c].astype(BF16)
        put(g_s.at[s], g_h.at[s])
        g = g_s[s]
        l, r = split(bs[s]), split(bs[2 + s])
        t = split(dot2l(l, g, 0, 0))
        rot = clip * dot3(t, r, 1, 0)
        v = KEEP * vs[s] + MIX * rot * rot
        ratio = (KEEP * rots[s] + MIX * rot) / (jnp.sqrt(v) + STABILITY)
        rots[s] = rot
        put(rots.at[s], rot_h.at[s])
        step = dot3(split(dot3(l, split(ratio), 1, 0)), r, 1, 1)
        for c in range(4):
            x_s[c] = step[:, c * D:(c + 1) * D]
        for q in range(4):
            for c in range(4):
                steps[pl.ds(16 * s + 4 * q + c, devices, stride=32), :] = x_s[c, pl.ds(q, D, stride=4), :]
        p = ps[s] + weight * dot2(g, t, 1, 1)
        ps[s] = p
        put(ps.at[s], p_h.at[s])
        p = split(p)
        gram[s] = dot3(p, p, 0, 0)
        put(gram.at[s], a_h.at[s])
        p = ps[2 + s] + weight * dot2(g, split(dot2(g, r, 1, 0)), 0, 0)
        ps[2 + s] = p
        put(ps.at[2 + s], p_h.at[2 + s])
        p = split(p)
        gram[2 + s] = dot3(p, p, 0, 0)
        put(gram.at[2 + s], a_h.at[2 + s])
    put(steps, step_h)
    for s in range(2):
        pltpu.make_async_copy(arr.at[s, most], arr.at[s, most], send_sem.at[s]).wait()
    pltpu.make_async_copy(sqs.at[most], sqs.at[most], send_sem.at[2]).wait()
    for c in outs:
        c.wait()


def travel(code, gradient, left_stat, left_basis, right_stat, right_basis, moment, second):
    devices, mp = lax.axis_size(("dp", "mp")), lax.axis_size("mp")
    vm = pl.BlockSpec(memory_space=pltpu.VMEM)
    hb = pl.BlockSpec(memory_space=pl.ANY)
    four = jax.ShapeDtypeStruct((4, N, N), F32)
    two = jax.ShapeDtypeStruct((2, N, N), F32)
    return pl.pallas_call(
        functools.partial(travel_kernel, devices, mp),
        out_shape=[
            four, four, jax.ShapeDtypeStruct((2, N, N), BF16), two,
            jax.ShapeDtypeStruct((32 * devices, D), F32), jax.ShapeDtypeStruct((8, D), F32),
        ],
        in_specs=[vm, vm] + [hb] * 6,
        out_specs=[hb] * 5 + [vm],
        scratch_shapes=[
            pltpu.VMEM((2, 16 * devices, D), F32),
            pltpu.VMEM((2, devices, 16, D), BF16),
            pltpu.VMEM((2, devices, 16, D), BF16),
            pltpu.VMEM((1, 1, D), F32),
            pltpu.VMEM((devices, 1, D), F32),
            pltpu.VMEM((4, N, D), F32),
            pltpu.VMEM((4, N, N), F32),
            pltpu.VMEM((4, N, N), F32),
            pltpu.VMEM((2, N, N), F32),
            pltpu.VMEM((2, N, N), F32),
            pltpu.VMEM((2, N, N), BF16),
            pltpu.VMEM((4, N, N), F32),
            pltpu.VMEM((4, N, N), F32),
            pltpu.VMEM((2, N, N), F32),
            pltpu.VMEM((32 * devices, D), F32),
            pltpu.SemaphoreType.DMA((8,)),
            pltpu.SemaphoreType.DMA((13,)),
            pltpu.SemaphoreType.DMA((3,)),
            pltpu.SemaphoreType.DMA((3,)),
        ],
        compiler_params=pltpu.CompilerParams(
            vmem_limit_bytes=56 << 20, collective_id=0, has_side_effects=True
        ),
        cost_estimate=pl.CostEstimate(flops=70 * 2 * N**3, bytes_accessed=32 * N * N * 4, transcendentals=0),
        name="travel",
    )(code, gradient, left_stat, left_basis, right_stat, right_basis, moment, second)


def refresh_kernel(live, clip_ref, g_ref, a_h, p_h, rot_h, ls_h, rs_h, lb_h, rb_h, m_h, v_h,
                   nls_h, nrs_h, nlb_h, nrb_h, nm_h, nv_h,
                   a_ref, p_ref, q_ref, w_d, w_e, st, bs, mo, vs, rots, in_sem, out_sem, q_sem):
    two = lambda ref, n: ref.at[pl.ds(n, 2)]
    ins = [(a_h, a_ref), (p_h, p_ref), (lb_h, two(bs, 0)), (rb_h, two(bs, 2)), (ls_h, two(st, 0)), (rs_h, two(st, 2)),
           (m_h, mo), (v_h, vs), (rot_h, rots)]
    loads = [pltpu.make_async_copy(src, dst, in_sem.at[i]) for i, (src, dst) in enumerate(ins)]
    for c in loads:
        c.start()
    clip = clip_ref[0:1, 0:1]
    weight = (MIX / N) * clip * clip
    gram = lambda g, c: lax.dot_general(g, g, (((c,), (c,)), ((), ())), preferred_element_type=F32)
    stores = [pltpu.make_async_copy(src, dst, out_sem.at[i]) for i, (src, dst) in enumerate(
        [(two(st, 0), nls_h), (two(st, 2), nrs_h), (mo, nm_h), (vs, nv_h)])]
    eye = (lax.broadcasted_iota(jnp.int32, (D, D), 0) == lax.broadcasted_iota(jnp.int32, (D, D), 1)).astype(F32)
    columns = lambda b, o: pltpu.make_async_copy(
        q_ref.at[b, :, pl.ds(o, D)], (nlb_h if b < 2 else nrb_h).at[b % 2, :, pl.ds(o, D)], q_sem.at[b, o // D])
    loads[0].wait()

    def step(k, carry):
        at = pl.ds(pl.multiple_of(k * D, D), D)
        for b in range(4):
            w_d[b] = a_ref[b, at, at]
            w_e[b] = eye
        for s in range(D // LB):
            here = slice(s * LB, (s + 1) * LB)
            ws = leaf([(w_d[b, here, :], w_e[b, here, :]) for b in range(4)], s, LB)
            for b in range(4):
                rd, re = ws[b]
                w_e[b, here, :] = re
                if s < D // LB - 1:
                    low = slice((s + 1) * LB, D)
                    dh, dl = split(rd)
                    eh, el = split(re)
                    lhs = jnp.concatenate([dh, dh, dl], axis=0)
                    rhs_d = jnp.concatenate([dh, dl, dh], axis=0)
                    rhs_e = jnp.concatenate([eh, el, eh], axis=0)
                    dims = (((0,), (0,)), ((), ()))
                    ud = lax.dot_general(lhs, rhs_d, dims, preferred_element_type=F32)
                    ue = lax.dot_general(lhs, rhs_e, dims, preferred_element_type=F32)
                    w_d[b, low, :] = w_d[b, low, :] - ud[(s + 1) * LB:, :]
                    w_e[b, low, :] = w_e[b, low, :] - ue[(s + 1) * LB:, :]
        for kk in range(N // D):
            @pl.when(k == kk)
            def _():
                o = kk * D
                if kk == 0:
                    for c in loads[1:4]:
                        c.wait()
                for b in range(4):
                    x = split(w_e[b])
                    q = dot3(split(p_ref[b, :, o:o + D]), x, 1, 1)
                    q_ref[b, :, o:o + D] = jnp.where(live[b % 2] > 0, q, bs[b, :, o:o + D])
                    columns(b, o).start()
                    if kk < N // D - 1:
                        r = split(dot3(x, split(a_ref[b, o:o + D, o + D:]), 1, 0))
                        for i in range(o + D, N, D):
                            rows = [y[:, i - o - D:i - o] for y in r]
                            rest = [y[:, i - o - D:] for y in r]
                            a_ref[b, i:i + D, i:] = a_ref[b, i:i + D, i:] - dot3(rows, rest, 0, 0)
                        p_ref[b, :, o + D:] = p_ref[b, :, o + D:] - dot3(split(q), r, 1, 0)
                if kk < 2:
                    loads[4 + kk].wait()
                    for s in range(2):
                        old = st[2 * kk + s]
                        st[2 * kk + s] = jnp.where(live[s] > 0, KEEP * old + weight * gram(g_ref[s], 1 - kk), old)
                    stores[kk].start()
                if kk == 2:
                    for c in loads[6:]:
                        c.wait()
                    for s in range(2):
                        mo[s] = jnp.where(live[s] > 0, KEEP * mo[s] + (MIX * clip) * g_ref[s].astype(F32), mo[s])
                        vs[s] = jnp.where(live[s] > 0, KEEP * vs[s] + MIX * rots[s] * rots[s], vs[s])
                    stores[2].start()
                    stores[3].start()
        return carry

    lax.fori_loop(0, N // D, step, 0)
    for c in stores:
        c.wait()
    for b in range(4):
        for o in range(0, N, D):
            columns(b, o).wait()


def refresh(live, clip, g, a, p, rot, left_stat, right_stat, left_basis, right_basis, moment, second):
    vm = pl.BlockSpec(memory_space=pltpu.VMEM)
    hb = pl.BlockSpec(memory_space=pl.ANY)
    return pl.pallas_call(
        refresh_kernel,
        out_shape=[jax.ShapeDtypeStruct((2, N, N), F32)] * 6,
        in_specs=[pl.BlockSpec(memory_space=pltpu.SMEM)] + [vm] * 2 + [hb] * 9,
        out_specs=[hb] * 6,
        scratch_shapes=[
            pltpu.VMEM((4, N, N), F32),
            pltpu.VMEM((4, N, N), F32),
            pltpu.VMEM((4, N, N), F32),
            pltpu.VMEM((4, D, D), F32),
            pltpu.VMEM((4, D, D), F32),
            pltpu.VMEM((4, N, N), F32),
            pltpu.VMEM((4, N, N), F32),
            pltpu.VMEM((2, N, N), F32),
            pltpu.VMEM((2, N, N), F32),
            pltpu.VMEM((2, N, N), F32),
            pltpu.SemaphoreType.DMA((9,)),
            pltpu.SemaphoreType.DMA((4,)),
            pltpu.SemaphoreType.DMA((4, N // D)),
        ],
        compiler_params=pltpu.CompilerParams(vmem_limit_bytes=56 << 20),
        cost_estimate=pl.CostEstimate(flops=100 * 2 * N**3, bytes_accessed=30 * N * N * 4, transcendentals=0),
        name="refresh",
    )(live, clip, g, a, p, rot, left_stat, right_stat, left_basis, right_basis, moment, second)


def shards(
    gradient,
    owner_device,
    state_slot,
    left_stat,
    right_stat,
    left_basis,
    right_basis,
    moment,
    second_moment,
):
    devices = lax.axis_size(("dp", "mp"))
    slot_count = left_stat.shape[0]
    flat_piece = gradient.shape[1]
    my_index = lax.axis_index(("dp", "mp"))
    slot_code = state_slot * devices + owner_device
    live = jnp.any(
        (owner_device[None, :] == my_index)
        & (state_slot[None, :] == jnp.arange(slot_count, dtype=jnp.int32)[:, None]),
        axis=1,
    ).astype(jnp.int32)
    a, p, g, rot, steps, clip = travel(
        slot_code[None, :], gradient, left_stat, left_basis, right_stat, right_basis, moment, second_moment
    )
    steps = steps.reshape(devices, 32, D)
    backward = lax.all_to_all(steps, ("dp", "mp"), split_axis=0, concat_axis=0, tiled=True)
    new_left, new_right, new_left_basis, new_right_basis, new_moment, new_second = refresh(
        live, clip, g, a, p, rot, left_stat, right_stat, left_basis, right_basis, moment, second_moment
    )
    rows = backward.reshape(devices * slot_count, 16, D)
    direction = jnp.take(rows, owner_device * slot_count + state_slot, axis=0).reshape(-1, flat_piece)
    return (
        new_left,
        new_right,
        new_left_basis,
        new_right_basis,
        new_moment,
        new_second,
        direction,
    )


def solution(mesh):
    spread = P(("dp", "mp"), None, None)
    flat = P(None, ("dp", "mp"))
    return jax.shard_map(
        shards,
        mesh=mesh,
        in_specs=(flat, P(), P()) + (spread,) * 6,
        out_specs=(spread,) * 6 + (flat,),
        check_vma=False,
    )
```

```python
import functools

import jax
import jax.numpy as jnp
from jax import lax
from jax.experimental import pallas as pl
from jax.experimental.pallas import tpu as pltpu
from jax.sharding import PartitionSpec as P

N = 512
D = 128
LB = 16
PIECE = 2048
F32 = jnp.float32
BF16 = jnp.bfloat16
KEEP = 0.9
MIX = 1.0 - KEEP
STABILITY = 1e-08


def split(x):
    hi = x.astype(BF16)
    lo = (x - hi.astype(F32)).astype(BF16)
    return hi, lo


def dot3(a, b, ca, cb):
    dims = (((ca,), (cb,)), ((), ()))
    return lax.dot_general(jnp.concatenate([a[0], a[0], a[1]], axis=ca), jnp.concatenate([b[0], b[1], b[0]], axis=cb), dims, preferred_element_type=F32)


def leaf(ws, s, lb):
    n = len(ws)
    sub = lax.broadcasted_iota(jnp.int32, (8, D), 0)
    lane = lax.broadcasted_iota(jnp.int32, (8, D), 1)
    ng = lb // 8
    ws = [[w[8 * i:8 * i + 8] for i in range(ng)] for w in ws]
    pv = [[None] * ng for _ in range(n)]
    for g in range(ng):
        c0 = s * lb + 8 * g
        bc = [[[jnp.broadcast_to(w[i][:, c0 + j:c0 + j + 1], (8, D)) for i in range(g, ng)] for j in range(8)] for w in ws]
        for k in range(8):
            for b in range(n):
                w = ws[b]
                cols = bc[b]
                own = cols[k]
                p = jnp.broadcast_to(own[0][k:k + 1, :], (8, D))
                rp = 1.0 / p
                pv[b][g] = p if k == 0 else jnp.where(sub >= k, p, pv[b][g])
                m = [x * rp for x in own]
                m[0] = jnp.where(sub > k, m[0], 0.0)
                for j in range(k + 1, 8):
                    f = jnp.broadcast_to(own[0][j:j + 1, :], (8, D))
                    cols[j] = [x - y * f for x, y in zip(cols[j], m)]
                row = jnp.where(lane == c0 + k, 1.0, jnp.broadcast_to(w[g][k:k + 1, :], (8, D)))
                for i in range(g, ng):
                    if i == g and k == 7:
                        continue
                    w[i] = jnp.where(lane == c0 + k, 0.0, w[i]) - m[i - g] * row
    out = []
    for b in range(n):
        rows = []
        for g in range(ng):
            diag = sub + (s * lb + 8 * g)
            w = ws[b][g]
            w = jnp.where(lane == diag, 1.0, jnp.where((lane > diag) & (lane < (s + 1) * lb), 0.0, w))
            rows.append(w * lax.rsqrt(pv[b][g]))
        out.append(jnp.concatenate(rows, axis=0))
    return out


def dot2(a, b, ca, cb):
    dims = (((ca,), (cb,)), ((), ()))
    d = lambda x, y: lax.dot_general(x, y, dims, preferred_element_type=F32)
    return d(a, b[0]) + d(a, b[1])


def dot2l(a, b, ca, cb):
    dims = (((ca,), (cb,)), ((), ()))
    d = lambda x, y: lax.dot_general(x, y, dims, preferred_element_type=F32)
    return d(a[0], b) + d(a[1], b)


def travel_kernel(devices, mp, owner, slot, grad, ls_h, lb_h, rs_h, rb_h, m_h, v_h,
                  a_h, p_h, g_h, rot_h, step_h, clip_out,
                  stage, away, arr, sq, sqs, x_s, st, bs, mo, vs, g_s, ps, gram, rots, steps,
                  in_sem, out_sem, send_sem, recv_sem):
    me = lax.axis_index("dp") * mp + lax.axis_index("mp")
    place = lambda d: {"dp": lax.div(d, mp), "mp": lax.rem(d, mp)}
    barrier = pltpu.get_barrier_semaphore()

    def greet(i, carry):
        pl.semaphore_signal(barrier, inc=1, device_id=place(lax.rem(me + i, devices)), device_id_type=pl.DeviceIdType.MESH)
        return carry

    lax.fori_loop(1, devices, greet, 0)
    ins = [(lb_h, bs.at[pl.ds(0, 2)]), (ls_h, st.at[pl.ds(0, 2)]), (rb_h, bs.at[pl.ds(2, 2)]), (rs_h, st.at[pl.ds(2, 2)]), (m_h, mo), (v_h, vs)]
    loads = [pltpu.make_async_copy(src, dst, in_sem.at[n]) for n, (src, dst) in enumerate(ins)]
    for c in loads:
        c.start()

    g = grad[...]
    for s in range(2):
        names = lax.broadcasted_iota(jnp.int32, (devices, owner.shape[1]), 0)
        picker = ((names == owner[...]) & (slot[...] == s)).astype(BF16)
        row = jnp.dot(picker, g, preferred_element_type=F32)
        for r in range(16):
            stage[s, pl.ds(r, devices, stride=16), :] = row[:, r * D:(r + 1) * D]
        away[s] = stage[s].astype(BF16).reshape(devices, 16, D)
    gf = g.astype(F32)
    own = jnp.sum(jnp.sum(gf * gf, axis=1, keepdims=True), axis=0, keepdims=True)
    sq[0] = jnp.broadcast_to(own, (1, D))
    sqs[me] = sq[0]
    pl.semaphore_wait(barrier, devices - 1)

    def send(src, dst, n):
        def one(i, carry):
            to = lax.rem(me + i, devices)
            pltpu.make_async_remote_copy(
                src_ref=src(to), dst_ref=dst, send_sem=send_sem.at[n], recv_sem=recv_sem.at[n],
                device_id=place(to), device_id_type=pl.DeviceIdType.MESH,
            ).start()
            return carry

        lax.fori_loop(1, devices, one, 0)

    send(lambda to: away.at[0, to], arr.at[0, me], 0)
    send(lambda to: sq.at[0], sqs.at[me], 2)
    send(lambda to: away.at[1, to], arr.at[1, me], 1)
    keep = [pltpu.make_async_copy(away.at[s, me], arr.at[s, me], in_sem.at[6 + s]) for s in range(2)]
    for c in keep:
        c.start()

    for c in loads[:4]:
        c.wait()
    for b in range(4):
        ps[b] = KEEP * dot3(split(st[b]), split(bs[b]), 1, 0)
    loads[4].wait()
    for s in range(2):
        rots[s] = dot3(split(dot3(split(bs[s]), split(mo[s]), 0, 0)), split(bs[2 + s]), 1, 0)
    loads[5].wait()
    most = pl.ds(0, devices - 1)
    outs = []

    def put(src, dst):
        outs.append(pltpu.make_async_copy(src, dst, out_sem.at[len(outs)]))
        outs[-1].start()

    half = N // 2

    def upper(b, p):
        gram[b, :half] = dot3([y[:, :half] for y in p], p, 0, 0)
        gram[b, half:, :half] = jnp.zeros((half, half), F32)
        low = [y[:, half:] for y in p]
        gram[b, half:, half:] = dot3(low, low, 0, 0)

    for s in range(2):
        pltpu.make_async_copy(arr.at[s, most], arr.at[s, most], recv_sem.at[s]).wait()
        keep[s].wait()
        if s == 0:
            pltpu.make_async_copy(sqs.at[most], sqs.at[most], recv_sem.at[2]).wait()
            mean = jnp.sum(sqs[...], axis=0) / (80.0 * N * N)
            clips = 1.0 / jnp.maximum(1.0, jnp.sqrt(mean))
            clip_out[...] = jnp.broadcast_to(clips, (8, D))
            clip = clips[:, 0:1]
            weight = (MIX / N) * clip * clip
        stage[s] = arr[s].astype(F32).reshape(16 * devices, D)
        for q in range(4):
            for c in range(4):
                x_s[c, pl.ds(q, D, stride=4), :] = stage[s, pl.ds(4 * q + c, devices, stride=16), :]
        for c in range(4):
            g_s[s, :, c * D:(c + 1) * D] = x_s[c].astype(BF16)
        put(g_s.at[s], g_h.at[s])
        g = g_s[s]
        l, r = split(bs[s]), split(bs[2 + s])
        t = split(dot2l(l, g, 0, 0))
        rot = clip * dot3(t, r, 1, 0)
        v = KEEP * vs[s] + MIX * rot * rot
        ratio = (KEEP * rots[s] + MIX * rot) / (jnp.sqrt(v) + STABILITY)
        rots[s] = rot
        put(rots.at[s], rot_h.at[s])
        step = dot3(split(dot3(l, split(ratio), 1, 0)), r, 1, 1)
        for c in range(4):
            x_s[c] = step[:, c * D:(c + 1) * D]
        for q in range(4):
            for c in range(4):
                steps[pl.ds(16 * s + 4 * q + c, devices, stride=32), :] = x_s[c, pl.ds(q, D, stride=4), :]
        p = ps[s] + weight * dot2(g, t, 1, 1)
        ps[s] = p
        put(ps.at[s], p_h.at[s])
        p = split(p)
        upper(s, p)
        put(gram.at[s], a_h.at[s])
        p = ps[2 + s] + weight * dot2(g, split(dot2(g, r, 1, 0)), 0, 0)
        ps[2 + s] = p
        put(ps.at[2 + s], p_h.at[2 + s])
        p = split(p)
        upper(2 + s, p)
        put(gram.at[2 + s], a_h.at[2 + s])
    put(steps, step_h)
    for s in range(2):
        pltpu.make_async_copy(arr.at[s, most], arr.at[s, most], send_sem.at[s]).wait()
    pltpu.make_async_copy(sqs.at[most], sqs.at[most], send_sem.at[2]).wait()
    for c in outs:
        c.wait()


def travel(owner, slot, gradient, left_stat, left_basis, right_stat, right_basis, moment, second):
    devices, mp = lax.axis_size(("dp", "mp")), lax.axis_size("mp")
    vm = pl.BlockSpec(memory_space=pltpu.VMEM)
    hb = pl.BlockSpec(memory_space=pl.ANY)
    four = jax.ShapeDtypeStruct((4, N, N), F32)
    two = jax.ShapeDtypeStruct((2, N, N), F32)
    return pl.pallas_call(
        functools.partial(travel_kernel, devices, mp),
        out_shape=[
            four, four, jax.ShapeDtypeStruct((2, N, N), BF16), two,
            jax.ShapeDtypeStruct((32 * devices, D), F32), jax.ShapeDtypeStruct((8, D), F32),
        ],
        in_specs=[vm] * 3 + [hb] * 6,
        out_specs=[hb] * 5 + [vm],
        scratch_shapes=[
            pltpu.VMEM((2, 16 * devices, D), F32),
            pltpu.VMEM((2, devices, 16, D), BF16),
            pltpu.VMEM((2, devices, 16, D), BF16),
            pltpu.VMEM((1, 1, D), F32),
            pltpu.VMEM((devices, 1, D), F32),
            pltpu.VMEM((4, N, D), F32),
            pltpu.VMEM((4, N, N), F32),
            pltpu.VMEM((4, N, N), F32),
            pltpu.VMEM((2, N, N), F32),
            pltpu.VMEM((2, N, N), F32),
            pltpu.VMEM((2, N, N), BF16),
            pltpu.VMEM((4, N, N), F32),
            pltpu.VMEM((4, N, N), F32),
            pltpu.VMEM((2, N, N), F32),
            pltpu.VMEM((32 * devices, D), F32),
            pltpu.SemaphoreType.DMA((8,)),
            pltpu.SemaphoreType.DMA((13,)),
            pltpu.SemaphoreType.DMA((3,)),
            pltpu.SemaphoreType.DMA((3,)),
        ],
        compiler_params=pltpu.CompilerParams(
            vmem_limit_bytes=56 << 20, collective_id=0, has_side_effects=True
        ),
        cost_estimate=pl.CostEstimate(flops=70 * 2 * N**3, bytes_accessed=32 * N * N * 4, transcendentals=0),
        name="travel",
    )(owner, slot, gradient, left_stat, left_basis, right_stat, right_basis, moment, second)


def refresh_kernel(live, clip_ref, g_ref, a_h, p_h, rot_h, ls_h, rs_h, lb_h, rb_h, m_h, v_h,
                   nls_h, nrs_h, nlb_h, nrb_h, nm_h, nv_h,
                   a_ref, p_ref, q_ref, w_d, qs, rs, st, bs, mo, vs, rots, in_sem, out_sem, q_sem):
    two = lambda ref, n: ref.at[pl.ds(n, 2)]
    ins = [(a_h, a_ref), (p_h, p_ref), (lb_h, two(bs, 0)), (rb_h, two(bs, 2)), (ls_h, two(st, 0)), (rs_h, two(st, 2)),
           (m_h, mo), (v_h, vs), (rot_h, rots)]
    loads = [pltpu.make_async_copy(src, dst, in_sem.at[i]) for i, (src, dst) in enumerate(ins)]
    for c in loads:
        c.start()
    clip = clip_ref[0:1, 0:1]
    weight = (MIX / N) * clip * clip
    gram = lambda g, c: lax.dot_general(g, g, (((c,), (c,)), ((), ())), preferred_element_type=F32)
    stores = [pltpu.make_async_copy(src, dst, out_sem.at[i]) for i, (src, dst) in enumerate(
        [(two(st, 0), nls_h), (two(st, 2), nrs_h), (mo, nm_h), (vs, nv_h)])]
    lane = lax.broadcasted_iota(jnp.int32, (1, D), 1)
    parts = D // LB
    columns = lambda b, o: pltpu.make_async_copy(
        q_ref.at[b, :, pl.ds(o, D)], (nlb_h if b < 2 else nrb_h).at[b % 2, :, pl.ds(o, D)], q_sem.at[b, o // D])
    qs[...] = jnp.zeros_like(qs)
    rs[...] = jnp.zeros_like(rs)
    loads[0].wait()
    loads[1].wait()

    def step(k, carry):
        at = pl.ds(pl.multiple_of(k * D, D), D)
        for b in range(4):
            w_d[b] = a_ref[b, at, at]
        for s in range(parts):
            here = slice(s * LB, (s + 1) * LB)
            low = slice((s + 1) * LB, D)
            ws = leaf([w_d[b, here, :] for b in range(4)], s, LB)
            for b in range(4):
                if b * parts // 4 == s:
                    p_ref[b] = p_ref[b] - dot3((qs[0, b], qs[1, b]), (rs[0, b], rs[1, b]), 1, 0)
            for b in range(4):
                w_d[b, here, :] = jnp.where(lane < (s + 1) * LB, ws[b], 0.0)
                if s < parts - 1:
                    hi, lo = split(ws[b])
                    u = dot3((hi, lo), (hi, lo), 0, 0)
                    old = jnp.where((lane >= s * LB) & (lane < (s + 1) * LB), 0.0, w_d[b, low, :])
                    w_d[b, low, :] = old - u[(s + 1) * LB:, :]
        for kk in range(N // D):
            @pl.when(k == kk)
            def _():
                o = kk * D
                if kk == 0:
                    for c in loads[2:4]:
                        c.wait()
                for b in range(4):
                    x = split(w_d[b])
                    q = dot3(split(p_ref[b, :, o:o + D]), x, 1, 1)
                    q_ref[b, :, o:o + D] = jnp.where(live[b % 2] > 0, q, bs[b, :, o:o + D])
                    columns(b, o).start()
                    if kk < N // D - 1:
                        r = split(dot3(x, split(a_ref[b, o:o + D, o + D:]), 1, 0))
                        for i in range(o + D, N, D):
                            rows = [y[:, i - o - D:i - o] for y in r]
                            rest = [y[:, i - o - D:] for y in r]
                            a_ref[b, i:i + D, i:] = a_ref[b, i:i + D, i:] - dot3(rows, rest, 0, 0)
                        rs[0, b, :, o:o + D] = jnp.zeros((D, D), BF16)
                        rs[1, b, :, o:o + D] = jnp.zeros((D, D), BF16)
                        rs[0, b, :, o + D:], rs[1, b, :, o + D:] = r
                        qs[0, b], qs[1, b] = split(q)
                if kk < 2:
                    loads[4 + kk].wait()
                    for s in range(2):
                        old = st[2 * kk + s]
                        st[2 * kk + s] = jnp.where(live[s] > 0, KEEP * old + weight * gram(g_ref[s], 1 - kk), old)
                    stores[kk].start()
                if kk == 2:
                    for c in loads[6:]:
                        c.wait()
                    for s in range(2):
                        mo[s] = jnp.where(live[s] > 0, KEEP * mo[s] + (MIX * clip) * g_ref[s].astype(F32), mo[s])
                        vs[s] = jnp.where(live[s] > 0, KEEP * vs[s] + MIX * rots[s] * rots[s], vs[s])
                    stores[2].start()
                    stores[3].start()
        return carry

    lax.fori_loop(0, N // D, step, 0)
    for c in stores:
        c.wait()
    for b in range(4):
        for o in range(0, N, D):
            columns(b, o).wait()


def refresh(live, clip, g, a, p, rot, left_stat, right_stat, left_basis, right_basis, moment, second):
    vm = pl.BlockSpec(memory_space=pltpu.VMEM)
    hb = pl.BlockSpec(memory_space=pl.ANY)
    return pl.pallas_call(
        refresh_kernel,
        out_shape=[jax.ShapeDtypeStruct((2, N, N), F32)] * 6,
        in_specs=[pl.BlockSpec(memory_space=pltpu.SMEM)] + [vm] * 2 + [hb] * 9,
        out_specs=[hb] * 6,
        scratch_shapes=[
            pltpu.VMEM((4, N, N), F32),
            pltpu.VMEM((4, N, N), F32),
            pltpu.VMEM((4, N, N), F32),
            pltpu.VMEM((4, D, D), F32),
            pltpu.VMEM((2, 4, N, D), BF16),
            pltpu.VMEM((2, 4, D, N), BF16),
            pltpu.VMEM((4, N, N), F32),
            pltpu.VMEM((4, N, N), F32),
            pltpu.VMEM((2, N, N), F32),
            pltpu.VMEM((2, N, N), F32),
            pltpu.VMEM((2, N, N), F32),
            pltpu.SemaphoreType.DMA((9,)),
            pltpu.SemaphoreType.DMA((4,)),
            pltpu.SemaphoreType.DMA((4, N // D)),
        ],
        compiler_params=pltpu.CompilerParams(vmem_limit_bytes=56 << 20),
        cost_estimate=pl.CostEstimate(flops=100 * 2 * N**3, bytes_accessed=30 * N * N * 4, transcendentals=0),
        name="refresh",
    )(live, clip, g, a, p, rot, left_stat, right_stat, left_basis, right_basis, moment, second)


def shards(
    gradient,
    owner_device,
    state_slot,
    left_stat,
    right_stat,
    left_basis,
    right_basis,
    moment,
    second_moment,
):
    devices = lax.axis_size(("dp", "mp"))
    slot_count = left_stat.shape[0]
    flat_piece = gradient.shape[1]
    my_index = lax.axis_index(("dp", "mp"))
    live = jnp.any(
        (owner_device[None, :] == my_index)
        & (state_slot[None, :] == jnp.arange(slot_count, dtype=jnp.int32)[:, None]),
        axis=1,
    ).astype(jnp.int32)
    a, p, g, rot, steps, clip = travel(
        owner_device[None, :], state_slot[None, :], gradient, left_stat, left_basis, right_stat, right_basis, moment, second_moment
    )
    steps = steps.reshape(devices, 32, D)
    backward = lax.all_to_all(steps, ("dp", "mp"), split_axis=0, concat_axis=0, tiled=True)
    new_left, new_right, new_left_basis, new_right_basis, new_moment, new_second = refresh(
        live, clip, g, a, p, rot, left_stat, right_stat, left_basis, right_basis, moment, second_moment
    )
    rows = backward.reshape(devices * slot_count, 16, D)
    direction = jnp.take(rows, owner_device * slot_count + state_slot, axis=0).reshape(-1, flat_piece)
    return (
        new_left,
        new_right,
        new_left_basis,
        new_right_basis,
        new_moment,
        new_second,
        direction,
    )


def solution(mesh):
    spread = P(("dp", "mp"), None, None)
    flat = P(None, ("dp", "mp"))
    return jax.shard_map(
        shards,
        mesh=mesh,
        in_specs=(flat, P(), P()) + (spread,) * 6,
        out_specs=(spread,) * 6 + (flat,),
        check_vma=False,
    )
```

```python
import functools

import jax
import jax.numpy as jnp
from jax import lax
from jax.experimental import pallas as pl
from jax.experimental.pallas import tpu as pltpu
from jax.sharding import PartitionSpec as P

N = 512
D = 128
LB = 16
PIECE = 2048
F32 = jnp.float32
BF16 = jnp.bfloat16
KEEP = 0.9
MIX = 1.0 - KEEP
STABILITY = 1e-08


def split(x):
    hi = x.astype(BF16)
    lo = (x - hi.astype(F32)).astype(BF16)
    return hi, lo


def dot3(a, b, ca, cb):
    dims = (((ca,), (cb,)), ((), ()))
    return lax.dot_general(jnp.concatenate([a[0], a[0], a[1]], axis=ca), jnp.concatenate([b[0], b[1], b[0]], axis=cb), dims, preferred_element_type=F32)


def leaf(ws, s, lb):
    n = len(ws)
    sub = lax.broadcasted_iota(jnp.int32, (8, D), 0)
    lane = lax.broadcasted_iota(jnp.int32, (8, D), 1)
    ng = lb // 8
    ws = [[w[8 * i:8 * i + 8] for i in range(ng)] for w in ws]
    pv = [[None] * ng for _ in range(n)]
    for g in range(ng):
        c0 = s * lb + 8 * g
        bc = [[[jnp.broadcast_to(w[i][:, c0 + j:c0 + j + 1], (8, D)) for i in range(g, ng)] for j in range(8)] for w in ws]
        for k in range(8):
            for b in range(n):
                w = ws[b]
                cols = bc[b]
                own = cols[k]
                p = jnp.broadcast_to(own[0][k:k + 1, :], (8, D))
                rp = 1.0 / p
                pv[b][g] = p if k == 0 else jnp.where(sub >= k, p, pv[b][g])
                m = [x * rp for x in own]
                m[0] = jnp.where(sub > k, m[0], 0.0)
                for j in range(k + 1, 8):
                    f = jnp.broadcast_to(own[0][j:j + 1, :], (8, D))
                    cols[j] = [x - y * f for x, y in zip(cols[j], m)]
                row = jnp.where(lane == c0 + k, 1.0, jnp.broadcast_to(w[g][k:k + 1, :], (8, D)))
                for i in range(g, ng):
                    if i == g and k == 7:
                        continue
                    w[i] = jnp.where(lane == c0 + k, 0.0, w[i]) - m[i - g] * row
    out = []
    for b in range(n):
        rows = []
        for g in range(ng):
            diag = sub + (s * lb + 8 * g)
            w = ws[b][g]
            w = jnp.where(lane == diag, 1.0, jnp.where((lane > diag) & (lane < (s + 1) * lb), 0.0, w))
            rows.append(w * lax.rsqrt(pv[b][g]))
        out.append(jnp.concatenate(rows, axis=0))
    return out


def dot2(a, b, ca, cb):
    dims = (((ca,), (cb,)), ((), ()))
    d = lambda x, y: lax.dot_general(x, y, dims, preferred_element_type=F32)
    return d(a, b[0]) + d(a, b[1])


def dot2l(a, b, ca, cb):
    dims = (((ca,), (cb,)), ((), ()))
    d = lambda x, y: lax.dot_general(x, y, dims, preferred_element_type=F32)
    return d(a[0], b) + d(a[1], b)


def travel_kernel(devices, mp, owner, slot, grad, ls_h, lb_h, rs_h, rb_h, m_h, v_h,
                  a_h, p_h, g_h, rot_h, step_h, clip_out,
                  stage, away, arr, sq, sqs, x_s, st, bs, bh, bl, mo, vs, g_s, ps, gram, rots, steps,
                  in_sem, out_sem, send_sem, recv_sem):
    me = lax.axis_index("dp") * mp + lax.axis_index("mp")
    place = lambda d: {"dp": lax.div(d, mp), "mp": lax.rem(d, mp)}
    barrier = pltpu.get_barrier_semaphore()

    def greet(i, carry):
        pl.semaphore_signal(barrier, inc=1, device_id=place(lax.rem(me + i, devices)), device_id_type=pl.DeviceIdType.MESH)
        return carry

    lax.fori_loop(1, devices, greet, 0)
    ins = [(lb_h, bs.at[pl.ds(0, 2)]), (ls_h, st.at[pl.ds(0, 2)]), (rb_h, bs.at[pl.ds(2, 2)]), (rs_h, st.at[pl.ds(2, 2)]), (m_h, mo), (v_h, vs)]
    loads = [pltpu.make_async_copy(src, dst, in_sem.at[n]) for n, (src, dst) in enumerate(ins)]
    for c in loads:
        c.start()

    g = grad[...]
    for s in range(2):
        names = lax.broadcasted_iota(jnp.int32, (devices, owner.shape[1]), 0)
        picker = ((names == owner[...]) & (slot[...] == s)).astype(BF16)
        row = jnp.dot(picker, g, preferred_element_type=F32)
        for r in range(16):
            stage[s, pl.ds(r, devices, stride=16), :] = row[:, r * D:(r + 1) * D]
        away[s] = stage[s].astype(BF16).reshape(devices, 16, D)
    gf = g.astype(F32)
    own = jnp.sum(jnp.sum(gf * gf, axis=1, keepdims=True), axis=0, keepdims=True)
    sq[0] = jnp.broadcast_to(own, (1, D))
    sqs[me] = sq[0]
    pl.semaphore_wait(barrier, devices - 1)

    def one(src, dst, n, to):
        pltpu.make_async_remote_copy(
            src_ref=src, dst_ref=dst, send_sem=send_sem.at[n], recv_sem=recv_sem.at[n],
            device_id=place(to), device_id_type=pl.DeviceIdType.MESH,
        ).start()

    def send_first(i, carry):
        to = lax.rem(me + i, devices)
        one(away.at[0, to], arr.at[0, me], 0, to)
        return carry

    def send_second(i):
        to = lax.rem(me + i, devices)
        one(sq.at[0], sqs.at[me], 2, to)
        one(away.at[1, to], arr.at[1, me], 1, to)

    lax.fori_loop(1, devices, send_first, 0)
    keep = [pltpu.make_async_copy(away.at[s, me], arr.at[s, me], in_sem.at[6 + s]) for s in range(2)]
    for c in keep:
        c.start()

    for c in loads[:4]:
        c.wait()
    for b in range(4):
        bh[b], bl[b] = split(bs[b])

    tiles = N // D
    each = devices // (4 * tiles)

    def tile_of(n):
        b = lax.div(n, tiles)
        at = pl.ds(pl.multiple_of(lax.rem(n, tiles) * D, D), D)
        ps[b, at, :] = KEEP * dot3(split(st[b, at, :]), (bh[b], bl[b]), 1, 0)

    def send_and_tile(n, carry):
        for u in range(each):
            send_second(each * n + each + u)
        tile_of(n)
        return carry

    for i in range(1, each):
        send_second(i)
    lax.fori_loop(0, 4 * tiles - 1, send_and_tile, 0)
    ps[3, N - D:, :] = KEEP * dot3(split(st[3, N - D:, :]), (bh[3], bl[3]), 1, 0)
    loads[4].wait()
    for s in range(2):
        rots[s] = dot3(split(dot3((bh[s], bl[s]), split(mo[s]), 0, 0)), (bh[2 + s], bl[2 + s]), 1, 0)
    loads[5].wait()
    most = pl.ds(0, devices - 1)
    outs = []

    def put(src, dst):
        outs.append(pltpu.make_async_copy(src, dst, out_sem.at[len(outs)]))
        outs[-1].start()

    half = N // 2

    def upper(b, p):
        gram[b, :half] = dot3([y[:, :half] for y in p], p, 0, 0)
        gram[b, half:, :half] = jnp.zeros((half, half), F32)
        low = [y[:, half:] for y in p]
        gram[b, half:, half:] = dot3(low, low, 0, 0)

    for s in range(2):
        pltpu.make_async_copy(arr.at[s, most], arr.at[s, most], recv_sem.at[s]).wait()
        keep[s].wait()
        if s == 0:
            pltpu.make_async_copy(sqs.at[most], sqs.at[most], recv_sem.at[2]).wait()
            mean = jnp.sum(sqs[...], axis=0) / (80.0 * N * N)
            clips = 1.0 / jnp.maximum(1.0, jnp.sqrt(mean))
            clip_out[...] = jnp.broadcast_to(clips, (8, D))
            clip = clips[:, 0:1]
            weight = (MIX / N) * clip * clip
        stage[s] = arr[s].astype(F32).reshape(16 * devices, D)
        for q in range(4):
            for c in range(4):
                x_s[c, pl.ds(q, D, stride=4), :] = stage[s, pl.ds(4 * q + c, devices, stride=16), :]
        for c in range(4):
            g_s[s, :, c * D:(c + 1) * D] = x_s[c].astype(BF16)
        put(g_s.at[s], g_h.at[s])
        g = g_s[s]
        l, r = (bh[s], bl[s]), (bh[2 + s], bl[2 + s])
        t = split(dot2l(l, g, 0, 0))
        rot = clip * dot3(t, r, 1, 0)
        v = KEEP * vs[s] + MIX * rot * rot
        ratio = (KEEP * rots[s] + MIX * rot) / (jnp.sqrt(v) + STABILITY)
        rots[s] = rot
        put(rots.at[s], rot_h.at[s])
        step = dot3(split(dot3(l, split(ratio), 1, 0)), r, 1, 1)
        for c in range(4):
            x_s[c] = step[:, c * D:(c + 1) * D]
        for q in range(4):
            for c in range(4):
                steps[pl.ds(16 * s + 4 * q + c, devices, stride=32), :] = x_s[c, pl.ds(q, D, stride=4), :]
        p = ps[s] + weight * dot2(g, t, 1, 1)
        ps[s] = p
        put(ps.at[s], p_h.at[s])
        p = split(p)
        upper(s, p)
        put(gram.at[s], a_h.at[s])
        p = ps[2 + s] + weight * dot2(g, split(dot2(g, r, 1, 0)), 0, 0)
        ps[2 + s] = p
        put(ps.at[2 + s], p_h.at[2 + s])
        p = split(p)
        upper(2 + s, p)
        put(gram.at[2 + s], a_h.at[2 + s])
    put(steps, step_h)
    for s in range(2):
        pltpu.make_async_copy(arr.at[s, most], arr.at[s, most], send_sem.at[s]).wait()
    pltpu.make_async_copy(sqs.at[most], sqs.at[most], send_sem.at[2]).wait()
    for c in outs:
        c.wait()


def travel(owner, slot, gradient, left_stat, left_basis, right_stat, right_basis, moment, second):
    devices, mp = lax.axis_size(("dp", "mp")), lax.axis_size("mp")
    vm = pl.BlockSpec(memory_space=pltpu.VMEM)
    hb = pl.BlockSpec(memory_space=pl.ANY)
    four = jax.ShapeDtypeStruct((4, N, N), F32)
    two = jax.ShapeDtypeStruct((2, N, N), F32)
    return pl.pallas_call(
        functools.partial(travel_kernel, devices, mp),
        out_shape=[
            four, four, jax.ShapeDtypeStruct((2, N, N), BF16), two,
            jax.ShapeDtypeStruct((32 * devices, D), F32), jax.ShapeDtypeStruct((8, D), F32),
        ],
        in_specs=[vm] * 3 + [hb] * 6,
        out_specs=[hb] * 5 + [vm],
        scratch_shapes=[
            pltpu.VMEM((2, 16 * devices, D), F32),
            pltpu.VMEM((2, devices, 16, D), BF16),
            pltpu.VMEM((2, devices, 16, D), BF16),
            pltpu.VMEM((1, 1, D), F32),
            pltpu.VMEM((devices, 1, D), F32),
            pltpu.VMEM((4, N, D), F32),
            pltpu.VMEM((4, N, N), F32),
            pltpu.VMEM((4, N, N), F32),
            pltpu.VMEM((4, N, N), BF16),
            pltpu.VMEM((4, N, N), BF16),
            pltpu.VMEM((2, N, N), F32),
            pltpu.VMEM((2, N, N), F32),
            pltpu.VMEM((2, N, N), BF16),
            pltpu.VMEM((4, N, N), F32),
            pltpu.VMEM((4, N, N), F32),
            pltpu.VMEM((2, N, N), F32),
            pltpu.VMEM((32 * devices, D), F32),
            pltpu.SemaphoreType.DMA((8,)),
            pltpu.SemaphoreType.DMA((13,)),
            pltpu.SemaphoreType.DMA((3,)),
            pltpu.SemaphoreType.DMA((3,)),
        ],
        compiler_params=pltpu.CompilerParams(
            vmem_limit_bytes=56 << 20, collective_id=0, has_side_effects=True
        ),
        cost_estimate=pl.CostEstimate(flops=70 * 2 * N**3, bytes_accessed=32 * N * N * 4, transcendentals=0),
        name="travel",
    )(owner, slot, gradient, left_stat, left_basis, right_stat, right_basis, moment, second)


def refresh_kernel(live, clip_ref, g_ref, a_h, p_h, rot_h, ls_h, rs_h, lb_h, rb_h, m_h, v_h,
                   nls_h, nrs_h, nlb_h, nrb_h, nm_h, nv_h,
                   a_ref, p_ref, q_ref, w_d, qs, rs, st, bs, mo, vs, rots, in_sem, out_sem, q_sem):
    two = lambda ref, n: ref.at[pl.ds(n, 2)]
    ins = [(a_h, a_ref), (p_h, p_ref), (lb_h, two(bs, 0)), (rb_h, two(bs, 2)), (ls_h, two(st, 0)), (rs_h, two(st, 2)),
           (m_h, mo), (v_h, vs), (rot_h, rots)]
    loads = [pltpu.make_async_copy(src, dst, in_sem.at[i]) for i, (src, dst) in enumerate(ins)]
    for c in loads:
        c.start()
    clip = clip_ref[0:1, 0:1]
    weight = (MIX / N) * clip * clip
    gram = lambda g, c: lax.dot_general(g, g, (((c,), (c,)), ((), ())), preferred_element_type=F32)
    stores = [pltpu.make_async_copy(src, dst, out_sem.at[i]) for i, (src, dst) in enumerate(
        [(two(st, 0), nls_h), (two(st, 2), nrs_h), (mo, nm_h), (vs, nv_h)])]
    lane = lax.broadcasted_iota(jnp.int32, (1, D), 1)
    parts = D // LB
    columns = lambda b, o: pltpu.make_async_copy(
        q_ref.at[b, :, pl.ds(o, D)], (nlb_h if b < 2 else nrb_h).at[b % 2, :, pl.ds(o, D)], q_sem.at[b, o // D])
    qs[...] = jnp.zeros_like(qs)
    rs[...] = jnp.zeros_like(rs)
    loads[0].wait()

    def step(k, carry):
        at = pl.ds(pl.multiple_of(k * D, D), D)
        for b in range(4):
            w_d[b] = a_ref[b, at, at]
        for s in range(parts):
            here = slice(s * LB, (s + 1) * LB)
            low = slice((s + 1) * LB, D)
            ws = leaf([w_d[b, here, :] for b in range(4)], s, LB)
            if s == 0:
                @pl.when(k == 0)
                def _():
                    loads[1].wait()

            for b in range(4):
                if b * parts // 4 == s - 1:
                    p_ref[b] = p_ref[b] - dot3((qs[0, b], qs[1, b]), (rs[0, b], rs[1, b]), 1, 0)
            for b in range(4):
                w_d[b, here, :] = jnp.where(lane < (s + 1) * LB, ws[b], 0.0)
                if s < parts - 1:
                    hi, lo = split(ws[b])
                    u = dot3((hi, lo), (hi, lo), 0, 0)
                    old = jnp.where((lane >= s * LB) & (lane < (s + 1) * LB), 0.0, w_d[b, low, :])
                    w_d[b, low, :] = old - u[(s + 1) * LB:, :]
        for kk in range(N // D):
            @pl.when(k == kk)
            def _():
                o = kk * D
                if kk == 0:
                    for c in loads[2:4]:
                        c.wait()
                for b in range(4):
                    x = split(w_d[b])
                    q = dot3(split(p_ref[b, :, o:o + D]), x, 1, 1)
                    q_ref[b, :, o:o + D] = jnp.where(live[b % 2] > 0, q, bs[b, :, o:o + D])
                    columns(b, o).start()
                    if kk < N // D - 1:
                        r = split(dot3(x, split(a_ref[b, o:o + D, o + D:]), 1, 0))
                        for i in range(o + D, N, D):
                            rows = [y[:, i - o - D:i - o] for y in r]
                            rest = [y[:, i - o - D:] for y in r]
                            a_ref[b, i:i + D, i:] = a_ref[b, i:i + D, i:] - dot3(rows, rest, 0, 0)
                        rs[0, b, :, o:o + D] = jnp.zeros((D, D), BF16)
                        rs[1, b, :, o:o + D] = jnp.zeros((D, D), BF16)
                        rs[0, b, :, o + D:], rs[1, b, :, o + D:] = r
                        qs[0, b], qs[1, b] = split(q)
                if kk < 2:
                    loads[4 + kk].wait()
                    for s in range(2):
                        old = st[2 * kk + s]
                        st[2 * kk + s] = jnp.where(live[s] > 0, KEEP * old + weight * gram(g_ref[s], 1 - kk), old)
                    stores[kk].start()
                if kk == 2:
                    for c in loads[6:]:
                        c.wait()
                    for s in range(2):
                        mo[s] = jnp.where(live[s] > 0, KEEP * mo[s] + (MIX * clip) * g_ref[s].astype(F32), mo[s])
                        vs[s] = jnp.where(live[s] > 0, KEEP * vs[s] + MIX * rots[s] * rots[s], vs[s])
                    stores[2].start()
                    stores[3].start()
        return carry

    lax.fori_loop(0, N // D, step, 0)
    for c in stores:
        c.wait()
    for b in range(4):
        for o in range(0, N, D):
            columns(b, o).wait()


def refresh(live, clip, g, a, p, rot, left_stat, right_stat, left_basis, right_basis, moment, second):
    vm = pl.BlockSpec(memory_space=pltpu.VMEM)
    hb = pl.BlockSpec(memory_space=pl.ANY)
    return pl.pallas_call(
        refresh_kernel,
        out_shape=[jax.ShapeDtypeStruct((2, N, N), F32)] * 6,
        in_specs=[pl.BlockSpec(memory_space=pltpu.SMEM)] + [vm] * 2 + [hb] * 9,
        out_specs=[hb] * 6,
        scratch_shapes=[
            pltpu.VMEM((4, N, N), F32),
            pltpu.VMEM((4, N, N), F32),
            pltpu.VMEM((4, N, N), F32),
            pltpu.VMEM((4, D, D), F32),
            pltpu.VMEM((2, 4, N, D), BF16),
            pltpu.VMEM((2, 4, D, N), BF16),
            pltpu.VMEM((4, N, N), F32),
            pltpu.VMEM((4, N, N), F32),
            pltpu.VMEM((2, N, N), F32),
            pltpu.VMEM((2, N, N), F32),
            pltpu.VMEM((2, N, N), F32),
            pltpu.SemaphoreType.DMA((9,)),
            pltpu.SemaphoreType.DMA((4,)),
            pltpu.SemaphoreType.DMA((4, N // D)),
        ],
        compiler_params=pltpu.CompilerParams(vmem_limit_bytes=56 << 20),
        cost_estimate=pl.CostEstimate(flops=100 * 2 * N**3, bytes_accessed=30 * N * N * 4, transcendentals=0),
        name="refresh",
    )(live, clip, g, a, p, rot, left_stat, right_stat, left_basis, right_basis, moment, second)


def shards(
    gradient,
    owner_device,
    state_slot,
    left_stat,
    right_stat,
    left_basis,
    right_basis,
    moment,
    second_moment,
):
    devices = lax.axis_size(("dp", "mp"))
    slot_count = left_stat.shape[0]
    flat_piece = gradient.shape[1]
    my_index = lax.axis_index(("dp", "mp"))
    live = jnp.any(
        (owner_device[None, :] == my_index)
        & (state_slot[None, :] == jnp.arange(slot_count, dtype=jnp.int32)[:, None]),
        axis=1,
    ).astype(jnp.int32)
    a, p, g, rot, steps, clip = travel(
        owner_device[None, :], state_slot[None, :], gradient, left_stat, left_basis, right_stat, right_basis, moment, second_moment
    )
    steps = steps.reshape(devices, 32, D)
    backward = lax.all_to_all(steps, ("dp", "mp"), split_axis=0, concat_axis=0, tiled=True)
    new_left, new_right, new_left_basis, new_right_basis, new_moment, new_second = refresh(
        live, clip, g, a, p, rot, left_stat, right_stat, left_basis, right_basis, moment, second_moment
    )
    rows = backward.reshape(devices * slot_count, 16, D)
    direction = jnp.take(rows, owner_device * slot_count + state_slot, axis=0).reshape(-1, flat_piece)
    return (
        new_left,
        new_right,
        new_left_basis,
        new_right_basis,
        new_moment,
        new_second,
        direction,
    )


def solution(mesh):
    spread = P(("dp", "mp"), None, None)
    flat = P(None, ("dp", "mp"))
    return jax.shard_map(
        shards,
        mesh=mesh,
        in_specs=(flat, P(), P()) + (spread,) * 6,
        out_specs=(spread,) * 6 + (flat,),
        check_vma=False,
    )
```
